256 devices in a mesh: band: 8 (over y, z_lo), dir: 32 (over z_hi, x, core).
Axes of the slice: x: 4, y: 4, z: 8 (z_hi: 4, z_lo: 2; z = z_hi * 2 + z_lo), core: 2. Of those that a mesh axis runs over, the one named last changes fastest.
Arguments:
- responses: bfloat16 [8, 32, 2, 512, 1536], P('band', 'dir'), may hold values from -0.15625 to 0.15625
- fluxes: float32 [8, 32, 1536], P('band', 'dir'), may hold values from 0.1 to 1.5
- counts: int32 [32], P('dir'), may hold values from 512 to 1536, as said below
- penalty: float32 [32], replicated, may hold values from 0.3 to 3
- visibilities: float32 [8, 2, 512, 512], P('band', None, 'dir'), may hold values from -3 to 3
- start_gains: float32 [8, 2, 32, 512], P('band', None, None, 'dir'), may hold values from 0.5 to 1.5
Outputs:
- gains: float32 [8, 2, 32, 512], P('band', None, None, 'dir')
- coefficients: float32 [3, 2, 32, 512], P(None, None, None, 'dir')
- residual: float32 [8, 2, 512, 512], P('band', None, 'dir')
The draws below stay inside these ranges and needn't reach their ends.
Inputs may be any that keep to these rules, and one draw needn't show every extreme that they name: `counts`: every direction has at least 512 live source slots, and some direction has exactly 1536.
All inputs are finite; a program needn't handle non-finite values.
Results may differ from the reference program's by a relative error of at most 0.0024.
Values may be sent and summed in bfloat16 or wider, within the bound.
A program may use at most 64 MiB of HBM per device.

```python
import math
import jax
import jax.numpy as jnp
from jax import lax

STATIONS = 512
SRC_MAX = 1536
SWEEPS = 3
BANDS = 8
DIRS = 32


def draw_counts(key, part):
    drawn_counts = jax.random.randint(key, (DIRS,), STATIONS, SRC_MAX)
    chosen = jax.random.randint(jax.random.fold_in(key, 7), (), 0, DIRS)
    return jnp.where(jnp.arange(DIRS) == chosen, SRC_MAX, drawn_counts).astype(jnp.int32)


def block_scale(key, extent, pieces, least, top_value):
    level, own = 1.0, jax.random.fold_in(key, 6)
    for dim, parts in pieces:
        steps = jnp.exp(jax.random.uniform(jax.random.fold_in(own, dim), (parts,), jnp.float32, least / len(pieces), top_value / len(pieces)))
        level = level * jnp.repeat(steps, extent[dim] // parts).reshape([-1 if axis == dim else 1 for axis in range(len(extent))])
    return level


def centred(stream_key, dims, scale, bound, pieces=(), dtype=jnp.bfloat16):
    result = jax.random.normal(stream_key, dims, jnp.float32) * scale
    if len(pieces) > 0:
        result = block_scale(stream_key, dims, pieces, -0.22, 0.18) * result
    return jnp.clip(result, min=-bound, max=bound).astype(dtype)


def setup_inputs(seed: int = 0) -> dict:
    key_list = jax.random.split(jax.random.key(seed), 7)
    return {
        "responses": centred(key_list[0], (BANDS, DIRS, 2, STATIONS, SRC_MAX), SRC_MAX ** -0.5, 0.15625, ((0, 8), (1, 32))),
        "fluxes": jnp.clip(jnp.exp(math.log(1.5) - 2.7080502 * jax.random.uniform(key_list[1], (BANDS, DIRS, SRC_MAX), jnp.float32) ** block_scale(key_list[1], (BANDS, DIRS, SRC_MAX), ((0, 8), (1, 32)), -0.2, 0.2)), 0.1, 1.5),
        "counts": draw_counts(jax.random.fold_in(key_list[6], 71), 0),
        "penalty": jnp.clip(jnp.exp(jax.random.uniform(key_list[3], (DIRS,), jnp.float32, math.log(0.3), math.log(3.0))), 0.3, 3.0),
        "visibilities": centred(key_list[4], (BANDS, 2, STATIONS, STATIONS), 0.5, 3.0, ((0, 8), (2, 32)), jnp.float32),
        "start_gains": jnp.clip(0.5 + 1.0 * jax.random.uniform(key_list[5], (BANDS, 2, DIRS, STATIONS), jnp.float32) ** block_scale(key_list[5], (BANDS, 2, DIRS, STATIONS), ((0, 8), (3, 32)), -0.2, 0.2), 0.5, 1.5),
    }


RIDGE_WEIGHT = 0.25
DAMPING = 0.5


def gram_inverse(band_total):
    locations = [(2.0 * position + 1.0 - band_total) / band_total for position in range(band_total)]
    gram = [[sum(location ** (first_index + second_index) for location in locations) + (RIDGE_WEIGHT if first_index == second_index else 0.0) for second_index in range(3)] for first_index in range(3)]

    def cofactor(first_index, second_index):
        kept_rows = [index_value for index_value in range(3) if index_value != first_index]
        kept_cols = [index_value for index_value in range(3) if index_value != second_index]
        minor_value = gram[kept_rows[0]][kept_cols[0]] * gram[kept_rows[1]][kept_cols[1]] - gram[kept_rows[0]][kept_cols[1]] * gram[kept_rows[1]][kept_cols[0]]
        return minor_value if (first_index + second_index) % 2 == 0 else -minor_value

    determinant = sum(gram[0][column] * cofactor(0, column) for column in range(3))
    return [[cofactor(column, row_index) / determinant for column in range(3)] for row_index in range(3)]


def basis_terms(position, band_total):
    frequency = (2.0 * position + 1.0 - band_total) / band_total
    return [jnp.ones_like(frequency), frequency, frequency * frequency]


def coherency_of(response, source_flux, live_count):
    station_count = response.shape[1]
    source_count = response.shape[2]
    live_mask = jnp.arange(source_count) < live_count
    weight = jnp.where(live_mask, source_flux, 0.0).astype(jnp.float32)
    stacked = response.reshape(2 * station_count, source_count)
    scaled = (stacked.astype(jnp.float32) * weight[None, :]).astype(jnp.bfloat16)
    product = lax.dot_general(stacked.astype(jnp.float32), scaled.astype(jnp.float32), (((1,), (1,)), ((), ())), precision=lax.Precision.HIGHEST, preferred_element_type=jnp.float32)
    real_part = product[:station_count, :station_count] + product[station_count:, station_count:]
    imag_part = product[station_count:, :station_count] - product[:station_count, station_count:]
    return jnp.stack([real_part, imag_part]).astype(jnp.bfloat16)


def project(coherency, row_gains, column_gains):
    coh_real = coherency[:, 0].astype(jnp.float32)
    coh_imag = coherency[:, 1].astype(jnp.float32)
    column_real = column_gains[0][:, None, :]
    column_imag = column_gains[1][:, None, :]
    along_real = coh_real * column_real + coh_imag * column_imag
    along_imag = coh_imag * column_real - coh_real * column_imag
    row_real = row_gains[0][:, :, None]
    row_imag = row_gains[1][:, :, None]
    model_real = jnp.sum(row_real * along_real - row_imag * along_imag, axis=0)
    model_imag = jnp.sum(row_real * along_imag + row_imag * along_real, axis=0)
    return along_real, along_imag, model_real, model_imag


def solve(along_real, along_imag, resid_real, resid_imag, offdiag, row_gains, target, duals, penalty):
    weight_sum = jnp.sum((along_real * along_real + along_imag * along_imag) * offdiag[None], axis=2)
    numer_real = jnp.sum(resid_real[None] * along_real + resid_imag[None] * along_imag, axis=2) + row_gains[0] * weight_sum
    numer_imag = jnp.sum(resid_imag[None] * along_real - resid_real[None] * along_imag, axis=2) + row_gains[1] * weight_sum
    strength = penalty[:, None]
    solved_real = (numer_real + strength * (target[0] - duals[0])) / (weight_sum + strength)
    solved_imag = (numer_imag + strength * (target[1] - duals[1])) / (weight_sum + strength)
    solved = jnp.stack([solved_real, solved_imag])
    return row_gains + DAMPING * (solved - row_gains)


def reference(responses, fluxes, counts, penalty, visibilities, start_gains):
    flat_resp = responses.reshape(BANDS * DIRS, 2, STATIONS, SRC_MAX)
    flat_flux = fluxes.reshape(BANDS * DIRS, SRC_MAX)
    flat_count = jnp.tile(counts, BANDS)
    coherency = lax.map(lambda operands: coherency_of(operands[0], operands[1], operands[2]), (flat_resp, flat_flux, flat_count))
    coherency = coherency.reshape(BANDS, DIRS, 2, STATIONS, STATIONS)
    offdiag = (jnp.arange(STATIONS)[:, None] != jnp.arange(STATIONS)[None, :]).astype(jnp.float32)
    terms = basis_terms(jnp.arange(BANDS).astype(jnp.float32), float(BANDS))
    inverse = gram_inverse(BANDS)
    current = start_gains
    target = start_gains
    duals = jnp.zeros_like(start_gains)

    def band_update(operands):
        band_coh, band_vis, band_gains, band_target, band_duals = operands
        along_real, along_imag, model_real, model_imag = project(band_coh, band_gains, band_gains)
        resid_real = (band_vis[0] - model_real) * offdiag
        resid_imag = (band_vis[1] - model_imag) * offdiag
        return solve(along_real, along_imag, resid_real, resid_imag, offdiag, band_gains, band_target, band_duals, penalty)

    def band_residual(operands):
        band_coh, band_vis, band_gains = operands
        along_real, along_imag, model_real, model_imag = project(band_coh, band_gains, band_gains)
        return jnp.stack([(band_vis[0] - model_real) * offdiag, (band_vis[1] - model_imag) * offdiag])

    coefficients = jnp.zeros((3, 2, DIRS, STATIONS), jnp.float32)
    for repeat in range(SWEEPS):
        current = lax.map(band_update, (coherency, visibilities, current, target, duals))
        mixed = current + duals
        moments = [jnp.sum(term[:, None, None, None] * mixed, axis=0) for term in terms]
        coeff_list = [moments[0] * inverse[row_index][0] + moments[1] * inverse[row_index][1] + moments[2] * inverse[row_index][2] for row_index in range(3)]
        target = terms[0][:, None, None, None] * coeff_list[0] + terms[1][:, None, None, None] * coeff_list[1] + terms[2][:, None, None, None] * coeff_list[2]
        duals = duals + current - target
        coefficients = jnp.stack(coeff_list)
    residual = lax.map(band_residual, (coherency, visibilities, current))
    return current, coefficients, residual
```

```python
import functools

import jax
import jax.numpy as jnp
from jax import lax
from jax.experimental import pallas as pl
from jax.experimental.pallas import tpu as pltpu
from jax.sharding import PartitionSpec as P

MESH = pl.DeviceIdType.MESH
SWEEPS = 3
RIDGE_WEIGHT = 0.25
DAMPING = 0.5
SLABS = 4
PART = 32
GROUP = 8
NT = (((1,), (1,)), ((), ()))


def gram_inverse(band_total):
    locations = [(2.0 * position + 1.0 - band_total) / band_total for position in range(band_total)]
    gram = [
        [
            sum((location ** (first + second) for location in locations))
            + (RIDGE_WEIGHT if first == second else 0.0)
            for second in range(3)
        ]
        for first in range(3)
    ]

    def cofactor(first, second):
        rows = [index for index in range(3) if index != first]
        cols = [index for index in range(3) if index != second]
        minor = gram[rows[0]][cols[0]] * gram[rows[1]][cols[1]] - gram[rows[0]][cols[1]] * gram[rows[1]][cols[0]]
        return minor if (first + second) % 2 == 0 else -minor

    determinant = sum((gram[0][column] * cofactor(0, column) for column in range(3)))
    return [[cofactor(column, row) / determinant for column in range(3)] for row in range(3)]


def calibrate(
    n_band,
    n_dir,
    resp_any,
    flux_ref,
    count_ref,
    penalty_ref,
    vis_ref,
    start_ref,
    gains_ref,
    coeff_ref,
    resid_ref,
    resp,
    scaled,
    coh_out,
    coh_in,
    coh,
    along,
    columns,
    rows_wide,
    gain_out,
    gain_in,
    mixed_out,
    mixed_in,
    load_sem,
    coh_send,
    coh_recv,
    gain_send,
    gain_recv,
    mixed_send,
    mixed_recv,
):
    me = lax.axis_index("dir")
    band = lax.axis_index("band")
    stations, sources = resp.shape[1], resp.shape[2]
    per_slab = n_dir // SLABS
    own = stations // n_dir
    tiles = stations // 128
    slab_rows = stations // SLABS
    my_slab = me // per_slab
    my_place = lax.rem(me, per_slab)

    load = pltpu.make_async_copy(resp_any.at[0, 0], resp, load_sem)
    load.start()

    barrier = pltpu.get_barrier_semaphore()

    def greet_dir(step, carry):
        pl.semaphore_signal(
            barrier, inc=1, device_id=(band, lax.rem(me + step, n_dir)), device_id_type=MESH
        )
        return carry

    def greet_band(step, carry):
        pl.semaphore_signal(
            barrier, inc=1, device_id=(lax.rem(band + step, n_band), me), device_id_type=MESH
        )
        return carry

    lax.fori_loop(1, n_dir, greet_dir, 0)
    lax.fori_loop(1, n_band, greet_band, 0)

    lane = lax.broadcasted_iota(jnp.int32, (own, 128), 1)
    dir_lane = lane % PART
    part_lane = lane % (2 * PART)
    low_half = lane < 2 * PART
    fold = (
        lax.broadcasted_iota(jnp.int32, (2 * PART, 128), 0)
        == lax.broadcasted_iota(jnp.int32, (2 * PART, 128), 1) % (2 * PART)
    ).astype(jnp.bfloat16)

    def split(value):
        high = value.astype(jnp.bfloat16).astype(jnp.float32)
        return jnp.where(low_half, high, value - high).astype(jnp.bfloat16)

    def unpack(value):
        return lax.dot_general(fold, value, NT, preferred_element_type=jnp.float32)

    eye = (
        lax.broadcasted_iota(jnp.int32, (own, own), 0) == lax.broadcasted_iota(jnp.int32, (own, own), 1)
    ).astype(jnp.bfloat16)
    pieces = []
    for part in range(2):
        pieces.append(start_ref[0, part])
        if n_dir < PART:
            pieces.append(jnp.zeros((PART - n_dir, own), jnp.float32))
    stacked = jnp.concatenate(pieces + pieces, axis=0)
    first = stacked.astype(jnp.bfloat16)
    rest = stacked - first.astype(jnp.float32)
    second = rest.astype(jnp.bfloat16)
    third = (rest - second.astype(jnp.float32)).astype(jnp.bfloat16)
    gains = (
        lax.dot_general(eye, first, NT, preferred_element_type=jnp.float32)
        + lax.dot_general(eye, second, NT, preferred_element_type=jnp.float32)
    ) + lax.dot_general(eye, third, NT, preferred_element_type=jnp.float32)

    strength = jnp.ones((own, 128), jnp.float32)
    for index in range(n_dir):
        strength = jnp.where(dir_lane == index, penalty_ref[index], strength)

    row_id = lax.broadcasted_iota(jnp.int32, (own, stations), 0) + me * own
    col_id = lax.broadcasted_iota(jnp.int32, (own, stations), 1)
    vis_re = jnp.where(row_id == col_id, 0.0, vis_ref[0, 0])
    vis_im = jnp.where(row_id == col_id, 0.0, vis_ref[0, 1])

    def tile(value, index):
        return value[:, index * 128 : (index + 1) * 128]

    def widen(value):
        for part in range(2):
            for index in range(n_dir):
                place = part * PART + index
                rows_wide[place] = jnp.broadcast_to(value[:, place : place + 1], (own, 128))

    def send_gains(slot, value):
        gain_out[slot] = split(value)
        gain_in[slot, me] = gain_out[slot]

        def send(step, carry):
            peer = lax.rem(me + step, n_dir)
            pltpu.make_async_remote_copy(
                src_ref=gain_out.at[slot],
                dst_ref=gain_in.at[slot, me],
                send_sem=gain_send.at[slot],
                recv_sem=gain_recv.at[slot],
                device_id=(band, peer),
                device_id_type=MESH,
            ).start()
            return carry

        lax.fori_loop(1, n_dir, send, 0)

    def receive_gains(slot):
        whole = gain_in.at[slot, pl.ds(0, n_dir - 1)]
        pltpu.make_async_copy(whole, whole, gain_recv.at[slot]).wait()
        packed = gain_in[slot].reshape(n_dir * own, 128)
        columns[...] = unpack(packed).reshape(columns.shape)

    def send_mixed(slot, value):
        mixed_out[slot] = split(value)
        mixed_in[slot, band] = mixed_out[slot]

        def send(step, carry):
            peer = lax.rem(band + step, n_band)
            pltpu.make_async_remote_copy(
                src_ref=mixed_out.at[slot],
                dst_ref=mixed_in.at[slot, band],
                send_sem=mixed_send.at[slot],
                recv_sem=mixed_recv.at[slot],
                device_id=(peer, me),
                device_id_type=MESH,
            ).start()
            return carry

        lax.fori_loop(1, n_band, send, 0)

    inverse = gram_inverse(n_band)
    own_place = (2.0 * band.astype(jnp.float32) + 1.0 - n_band) / n_band

    def receive_mixed(slot):
        whole = mixed_in.at[slot, pl.ds(0, n_band - 1)]
        pltpu.make_async_copy(whole, whole, mixed_recv.at[slot]).wait()
        sums = [None, None, None]
        for index in range(n_band):
            place = (2.0 * index + 1.0 - n_band) / n_band
            value = mixed_in[slot, index].astype(jnp.float32)
            for order in range(3):
                term = value * (place**order)
                sums[order] = term if sums[order] is None else sums[order] + term
        moments = [value + pltpu.roll(value, 2 * PART, 1) for value in sums]
        return [
            moments[0] * inverse[row][0] + moments[1] * inverse[row][1] + moments[2] * inverse[row][2]
            for row in range(3)
        ]

    live = lax.broadcasted_iota(jnp.int32, (1, sources), 1) < count_ref[0]
    weight = jnp.where(live, flux_ref[0], 0.0)
    load.wait()
    chunk = 64

    def scale(step, carry):
        for part in range(2):
            begin = pl.multiple_of(step * chunk, chunk)
            block = resp[part, pl.ds(begin, chunk), :].astype(jnp.float32)
            scaled[pl.ds(pl.multiple_of(part * stations + begin, chunk), chunk), :] = (
                block * weight
            ).astype(jnp.bfloat16)
        return carry

    lax.fori_loop(0, stations // chunk, scale, 0)

    def slab_step(step, carry):
        slab = lax.rem(my_slab + 2 + 3 * step + 3 * (step // 2) + 2 * (step // 3), SLABS)
        begin = pl.multiple_of(slab * slab_rows, slab_rows)
        left = jnp.concatenate(
            [resp[0, pl.ds(begin, slab_rows), :], resp[1, pl.ds(begin, slab_rows), :]], axis=0
        )
        by_re = lax.dot_general(left, scaled[:stations], NT, preferred_element_type=jnp.float32)
        by_im = lax.dot_general(left, scaled[stations:], NT, preferred_element_type=jnp.float32)
        real = by_re[:slab_rows] + by_im[slab_rows:]
        imag = by_re[slab_rows:] - by_im[:slab_rows]
        off = (lax.broadcasted_iota(jnp.int32, (slab_rows, stations), 0) + begin) != (
            lax.broadcasted_iota(jnp.int32, (slab_rows, stations), 1)
        )
        shape = (per_slab, own, stations)
        first_dir = slab * per_slab
        coh_out[pl.ds(first_dir, per_slab), 0] = (
            jnp.where(off, real, 0.0).astype(jnp.bfloat16).reshape(shape)
        )
        coh_out[pl.ds(first_dir, per_slab), 1] = (
            jnp.where(off, imag, 0.0).astype(jnp.bfloat16).reshape(shape)
        )

        @pl.when(step == 0)
        def _():
            pl.semaphore_wait(barrier, n_dir + n_band - 2)
            send_gains(0, gains)

        def send(place, inner):
            peer = first_dir + lax.rem(my_place + place, per_slab)

            @pl.when(peer != me)
            def _():
                pltpu.make_async_remote_copy(
                    src_ref=coh_out.at[peer],
                    dst_ref=coh_in.at[me],
                    send_sem=coh_send,
                    recv_sem=coh_recv.at[me],
                    device_id=(band, peer),
                    device_id_type=MESH,
                ).start()

            return inner

        lax.fori_loop(0, per_slab, send, 0)
        return carry

    lax.fori_loop(0, SLABS, slab_step, 0)
    coh_in[me] = coh_out[me]

    zero = jnp.zeros((own, 128), jnp.float32)

    def project(arriving):
        def step(group, totals):
            out = list(totals)
            for member in range(GROUP):
                index = group * GROUP + member
                if arriving:

                    @pl.when(index != me)
                    def _(index=index):
                        block = coh_in.at[index]
                        pltpu.make_async_copy(block, block, coh_recv.at[index]).wait()

                    coh[index] = coh_in[index].astype(jnp.float32)
                row_re = rows_wide[index]
                row_im = rows_wide[PART + index]
                for place in range(tiles):
                    here = pl.ds(place * 128, 128)
                    coh_re = coh[index, 0, :, here]
                    coh_im = coh[index, 1, :, here]
                    col_re = columns[group, member : member + 1, here]
                    col_im = columns[PART // GROUP + group, member : member + 1, here]
                    along_re = coh_re * col_re + coh_im * col_im
                    along_im = coh_im * col_re - coh_re * col_im
                    along[index, 0, :, here] = along_re
                    along[index, 1, :, here] = along_im
                    out[2 * place] += row_re * along_re - row_im * along_im
                    out[2 * place + 1] += row_re * along_im + row_im * along_re
            return tuple(out)

        totals = lax.fori_loop(0, n_dir // GROUP, step, (zero,) * (2 * tiles))
        return (
            [tile(vis_re, place) - totals[2 * place] for place in range(tiles)],
            [tile(vis_im, place) - totals[2 * place + 1] for place in range(tiles)],
        )

    def reduce(residual_re, residual_im):
        def step(index, carry):
            numer, weights = carry
            total_re, total_im, total_weight = zero, zero, zero
            for place in range(tiles):
                here = pl.ds(place * 128, 128)
                along_re = along[index, 0, :, here]
                along_im = along[index, 1, :, here]
                total_weight += along_re * along_re + along_im * along_im
                total_re += residual_re[place] * along_re + residual_im[place] * along_im
                total_im += residual_im[place] * along_re - residual_re[place] * along_im
            sum_re = jnp.sum(total_re, axis=1, keepdims=True)
            sum_im = jnp.sum(total_im, axis=1, keepdims=True)
            sum_weight = jnp.sum(total_weight, axis=1, keepdims=True)
            numer = jnp.where(
                part_lane == index, sum_re, jnp.where(part_lane == PART + index, sum_im, numer)
            )
            weights = jnp.where(dir_lane == index, sum_weight, weights)
            return numer, weights

        return lax.fori_loop(0, n_dir, step, (zero, zero))

    target = gains
    duals = zero
    coefficients = None
    for sweep in range(SWEEPS):
        widen(gains)
        receive_gains(sweep)
        residual_re, residual_im = project(sweep == 0)
        numer, weights = reduce(residual_re, residual_im)
        if sweep > 0:
            coefficients = receive_mixed(sweep - 1)
            target = coefficients[0] + own_place * coefficients[1] + own_place * own_place * coefficients[2]
            duals = duals + gains - target
        solved = (numer + gains * weights + strength * (target - duals)) / (weights + strength)
        gains = gains + DAMPING * (solved - gains)
        send_gains(sweep + 1, gains)
        send_mixed(sweep, gains + duals)
    widen(gains)
    own_gains = unpack(gain_out[SWEEPS])
    for part in range(2):
        gains_ref[0, part] = own_gains[part * PART : part * PART + n_dir]
    receive_gains(SWEEPS)
    residual_re, residual_im = project(False)
    for place in range(tiles):
        here = pl.ds(place * 128, 128)
        resid_ref[0, 0, :, here] = residual_re[place]
        resid_ref[0, 1, :, here] = residual_im[place]
    coefficients = receive_mixed(SWEEPS - 1)
    for order in range(3):
        value = unpack(split(coefficients[order]))
        for part in range(2):
            coeff_ref[order, part] = value[part * PART : part * PART + n_dir]

    whole = coh_out.at[pl.ds(0, n_dir - 1)]
    pltpu.make_async_copy(whole, whole, coh_send).wait()
    for slot in range(SWEEPS + 1):
        whole = gain_in.at[slot, pl.ds(0, n_dir - 1)]
        pltpu.make_async_copy(whole, whole, gain_send.at[slot]).wait()
    for slot in range(SWEEPS):
        whole = mixed_in.at[slot, pl.ds(0, n_band - 1)]
        pltpu.make_async_copy(whole, whole, mixed_send.at[slot]).wait()


def on_device(n_band, n_dir, responses, fluxes, counts, penalty, visibilities, start_gains):
    stations, sources = responses.shape[3], responses.shape[4]
    own = stations // n_dir
    vmem = pl.BlockSpec(memory_space=pltpu.VMEM)
    smem = pl.BlockSpec(memory_space=pltpu.SMEM)
    bf16, f32 = jnp.bfloat16, jnp.float32
    return pl.pallas_call(
        functools.partial(calibrate, n_band, n_dir),
        out_shape=(
            jax.ShapeDtypeStruct((1, 2, n_dir, own), f32),
            jax.ShapeDtypeStruct((3, 2, n_dir, own), f32),
            jax.ShapeDtypeStruct((1, 2, own, stations), f32),
        ),
        in_specs=[pl.BlockSpec(memory_space=pl.ANY), vmem, smem, smem, vmem, vmem],
        out_specs=(vmem, vmem, vmem),
        scratch_shapes=[
            pltpu.VMEM((2, stations, sources), bf16),
            pltpu.VMEM((2 * stations, sources), bf16),
            pltpu.VMEM((n_dir, 2, own, stations), bf16),
            pltpu.VMEM((n_dir, 2, own, stations), bf16),
            pltpu.VMEM((n_dir, 2, own, stations), f32),
            pltpu.VMEM((n_dir, 2, own, stations), f32),
            pltpu.VMEM((2 * PART // GROUP, GROUP, stations), f32),
            pltpu.VMEM((2 * PART, own, 128), f32),
            pltpu.VMEM((SWEEPS + 1, own, 128), bf16),
            pltpu.VMEM((SWEEPS + 1, n_dir, own, 128), bf16),
            pltpu.VMEM((SWEEPS, own, 128), bf16),
            pltpu.VMEM((SWEEPS, n_band, own, 128), bf16),
            pltpu.SemaphoreType.DMA,
            pltpu.SemaphoreType.DMA,
            pltpu.SemaphoreType.DMA((n_dir,)),
            pltpu.SemaphoreType.DMA((SWEEPS + 1,)),
            pltpu.SemaphoreType.DMA((SWEEPS + 1,)),
            pltpu.SemaphoreType.DMA((SWEEPS,)),
            pltpu.SemaphoreType.DMA((SWEEPS,)),
        ],
        compiler_params=pltpu.CompilerParams(
            collective_id=0, has_side_effects=True, vmem_limit_bytes=40 * 1024 * 1024
        ),
    )(responses, fluxes, counts, penalty, visibilities, start_gains)


def solution(mesh):
    in_specs = (
        P("band", "dir", None, None, None),
        P("band", "dir", None),
        P("dir"),
        P(),
        P("band", None, "dir", None),
        P("band", None, None, "dir"),
    )
    out_specs = (
        P("band", None, None, "dir"),
        P(None, None, None, "dir"),
        P("band", None, "dir", None),
    )
    return jax.shard_map(
        functools.partial(on_device, mesh.shape["band"], mesh.shape["dir"]),
        mesh=mesh,
        in_specs=in_specs,
        out_specs=out_specs,
        check_vma=False,
    )
```

```python
import functools

import jax
import jax.numpy as jnp
from jax import lax
from jax.experimental import pallas as pl
from jax.experimental.pallas import tpu as pltpu
from jax.sharding import PartitionSpec as P

MESH = pl.DeviceIdType.MESH
SWEEPS = 3
RIDGE_WEIGHT = 0.25
DAMPING = 0.5
SLABS = 4
PART = 32
GROUP = 8
NT = (((1,), (1,)), ((), ()))


def gram_inverse(band_total):
    locations = [(2.0 * position + 1.0 - band_total) / band_total for position in range(band_total)]
    gram = [
        [
            sum((location ** (first + second) for location in locations))
            + (RIDGE_WEIGHT if first == second else 0.0)
            for second in range(3)
        ]
        for first in range(3)
    ]

    def cofactor(first, second):
        rows = [index for index in range(3) if index != first]
        cols = [index for index in range(3) if index != second]
        minor = gram[rows[0]][cols[0]] * gram[rows[1]][cols[1]] - gram[rows[0]][cols[1]] * gram[rows[1]][cols[0]]
        return minor if (first + second) % 2 == 0 else -minor

    determinant = sum((gram[0][column] * cofactor(0, column) for column in range(3)))
    return [[cofactor(column, row) / determinant for column in range(3)] for row in range(3)]


def calibrate(
    n_band,
    n_dir,
    resp_hbm,
    flux_hbm,
    count_ref,
    penalty_ref,
    vis_hbm,
    start_hbm,
    gains_ref,
    coeff_ref,
    resid_ref,
    resp,
    flux,
    vis,
    start,
    scaled,
    coh_out,
    coh_in,
    coh,
    along,
    columns,
    rows_wide,
    sums,
    gain_out,
    gain_in,
    mixed_out,
    mixed_in,
    load_sem,
    coh_send,
    coh_recv,
    gain_send,
    gain_recv,
    mixed_send,
    mixed_recv,
):
    me = lax.axis_index("dir")
    band = lax.axis_index("band")
    stations, sources = resp.shape[1], resp.shape[2]
    per_slab = n_dir // SLABS
    own = stations // n_dir
    tiles = SLABS
    width = stations // SLABS
    my_slab = me // per_slab
    my_place = lax.rem(me, per_slab)

    loads = [
        pltpu.make_async_copy(source, goal, load_sem.at[index])
        for index, (source, goal) in enumerate(
            (
                (start_hbm.at[0], start),
                (flux_hbm.at[0], flux),
                (resp_hbm.at[0, 0], resp),
                (vis_hbm.at[0], vis),
            )
        )
    ]
    for load in loads:
        load.start()

    barrier = pltpu.get_barrier_semaphore()

    rotations = [step for step in (4, 5, 2, 3, 6, 7, 1, 0) if step < per_slab]
    places = [my_place if step == 0 else lax.rem(my_place + step, per_slab) for step in rotations]
    peers = []
    for offset in (2, 1, 3, 0):
        slab = lax.rem(my_slab + offset, SLABS)
        for step, place in zip(rotations, places):
            if offset or step:
                peers.append(slab * per_slab + place)
    bands = [lax.rem(band + step, n_band) for step in range(1, n_band)]
    for peer in peers:
        pl.semaphore_signal(barrier, inc=1, device_id=(band, peer), device_id_type=MESH)
    for peer in bands:
        pl.semaphore_signal(barrier, inc=1, device_id=(peer, me), device_id_type=MESH)

    lane = lax.broadcasted_iota(jnp.int32, (own, 128), 1)
    dir_lane = lane % PART
    part_lane = lane % (2 * PART)
    low_half = lane < 2 * PART
    fold = (
        lax.broadcasted_iota(jnp.int32, (2 * PART, 128), 0)
        == lax.broadcasted_iota(jnp.int32, (2 * PART, 128), 1) % (2 * PART)
    ).astype(jnp.bfloat16)
    zero = jnp.zeros((own, 128), jnp.float32)

    def split(value):
        high = value.astype(jnp.bfloat16).astype(jnp.float32)
        return jnp.where(low_half, high, value - high).astype(jnp.bfloat16)

    strength = jnp.ones((own, 128), jnp.float32)
    for index in range(n_dir):
        strength = jnp.where(dir_lane == index, penalty_ref[index], strength)

    loads[0].wait()
    pieces = []
    for part in range(2):
        pieces.append(start[part])
        if n_dir < PART:
            pieces.append(jnp.zeros((own, PART - n_dir), jnp.float32))
    gains = jnp.concatenate(pieces + pieces, axis=1)

    near = [lax.rem(my_slab + offset, SLABS) for offset in (0, 1, 3, 2)]
    spans = [pl.ds(pl.multiple_of(slab * width, width), width) for slab in near]

    def widen(value):
        for part in range(2):
            for index in range(n_dir):
                place = part * PART + index
                rows_wide[place] = jnp.broadcast_to(value[:, place : place + 1], (own, 128))

    def send_gains(slot, value):
        gain_out[slot] = split(value)
        gain_in[slot, my_slab, my_place] = gain_out[slot]

        for peer in peers:
            pltpu.make_async_remote_copy(
                src_ref=gain_out.at[slot],
                dst_ref=gain_in.at[slot, my_slab, my_place],
                send_sem=gain_send.at[slot],
                recv_sem=gain_recv.at[slot, my_slab],
                device_id=(band, peer),
                device_id_type=MESH,
            ).start()

    def receive_tile(slot, order):
        slab = near[order]
        whole = gain_in.at[slot, slab, pl.ds(0, per_slab - 1 if order == 0 else per_slab)]
        pltpu.make_async_copy(whole, whole, gain_recv.at[slot, slab]).wait()
        packed = gain_in[slot, slab].reshape(width, 128)
        value = lax.dot_general(fold, packed, NT, preferred_element_type=jnp.float32)
        columns[order] = value.reshape(columns.shape[1:])

    def send_mixed(slot, value):
        mixed_out[slot] = split(value)
        mixed_in[slot, band] = mixed_out[slot]

        for peer in bands:
            pltpu.make_async_remote_copy(
                src_ref=mixed_out.at[slot],
                dst_ref=mixed_in.at[slot, band],
                send_sem=mixed_send.at[slot],
                recv_sem=mixed_recv.at[slot],
                device_id=(peer, me),
                device_id_type=MESH,
            ).start()

    inverse = gram_inverse(n_band)
    own_place = (2.0 * band.astype(jnp.float32) + 1.0 - n_band) / n_band

    def receive_mixed(slot):
        whole = mixed_in.at[slot, pl.ds(0, n_band - 1)]
        pltpu.make_async_copy(whole, whole, mixed_recv.at[slot]).wait()
        totals = [None, None, None]
        for index in range(n_band):
            place = (2.0 * index + 1.0 - n_band) / n_band
            value = mixed_in[slot, index].astype(jnp.float32)
            for order in range(3):
                term = value * (place**order)
                totals[order] = term if totals[order] is None else totals[order] + term
        moments = [value + pltpu.roll(value, 2 * PART, 1) for value in totals]
        return [
            moments[0] * inverse[row][0] + moments[1] * inverse[row][1] + moments[2] * inverse[row][2]
            for row in range(3)
        ]

    loads[1].wait()
    live = lax.broadcasted_iota(jnp.int32, (1, sources), 1) < count_ref[0]
    weight = jnp.where(live, flux[...], 0.0)
    loads[2].wait()
    chunk = 64

    def scale(step, carry):
        for part in range(2):
            begin = pl.multiple_of(step * chunk, chunk)
            block = resp[part, pl.ds(begin, chunk), :].astype(jnp.float32)
            scaled[pl.ds(pl.multiple_of(part * stations + begin, chunk), chunk), :] = (
                block * weight
            ).astype(jnp.bfloat16)
        return carry

    lax.fori_loop(0, stations // chunk, scale, 0)

    def slab_step(step, carry):
        slab = lax.rem(my_slab + 2 + 3 * step + 3 * (step // 2) + 2 * (step // 3), SLABS)
        begin = pl.multiple_of(slab * width, width)
        left = jnp.concatenate([resp[0, pl.ds(begin, width), :], resp[1, pl.ds(begin, width), :]], axis=0)
        by_re = lax.dot_general(left, scaled[:stations], NT, preferred_element_type=jnp.float32)
        by_im = lax.dot_general(left, scaled[stations:], NT, preferred_element_type=jnp.float32)
        real = by_re[:width] + by_im[width:]
        imag = by_re[width:] - by_im[:width]
        off = (lax.broadcasted_iota(jnp.int32, (width, stations), 0) + begin) != (
            lax.broadcasted_iota(jnp.int32, (width, stations), 1)
        )
        shape = (per_slab, own, stations)
        first_dir = slab * per_slab
        coh_out[pl.ds(first_dir, per_slab), 0] = jnp.where(off, real, 0.0).astype(jnp.bfloat16).reshape(shape)
        coh_out[pl.ds(first_dir, per_slab), 1] = jnp.where(off, imag, 0.0).astype(jnp.bfloat16).reshape(shape)

        @pl.when(step == 0)
        def _():
            pl.semaphore_wait(barrier, n_dir + n_band - 2)
            send_gains(0, gains)

        def send(place, inner):
            peer = first_dir + lax.rem(my_place + per_slab // 2 + place, per_slab)

            @pl.when(peer != me)
            def _():
                pltpu.make_async_remote_copy(
                    src_ref=coh_out.at[peer],
                    dst_ref=coh_in.at[me],
                    send_sem=coh_send,
                    recv_sem=coh_recv.at[me],
                    device_id=(band, peer),
                    device_id_type=MESH,
                ).start()

            return inner

        lax.fori_loop(0, per_slab, send, 0)
        return carry

    lax.fori_loop(0, SLABS, slab_step, 0)
    coh_in[me] = coh_out[me]
    widen(gains)
    loads[3].wait()
    row_id = lax.broadcasted_iota(jnp.int32, (own, stations), 0) + me * own
    col_id = lax.broadcasted_iota(jnp.int32, (own, stations), 1)
    for part in range(2):
        vis[part] = jnp.where(row_id == col_id, 0.0, vis[part])

    def advance(index, group, member, order, totals):
        here = pl.ds(order * width, width)
        coh_re = coh[index, 0, :, here]
        coh_im = coh[index, 1, :, here]
        col_re = columns[order, group, member : member + 1]
        col_im = columns[order, PART // GROUP + group, member : member + 1]
        row_re = rows_wide[index]
        row_im = rows_wide[PART + index]
        along_re = coh_re * col_re + coh_im * col_im
        along_im = coh_im * col_re - coh_re * col_im
        along[index, 0, :, here] = along_re
        along[index, 1, :, here] = along_im
        return (
            totals[0] + (row_re * along_re - row_im * along_im),
            totals[1] + (row_re * along_im + row_im * along_re),
        )

    def left_over(order, totals):
        return vis[0, :, spans[order]] - totals[0], vis[1, :, spans[order]] - totals[1]

    def project_first():
        def step(group, totals):
            for member in range(GROUP):
                index = group * GROUP + member

                @pl.when(index != me)
                def _(index=index):
                    block = coh_in.at[index]
                    pltpu.make_async_copy(block, block, coh_recv.at[index]).wait()

                for order in range(tiles):
                    here = pl.ds(order * width, width)
                    for part in range(2):
                        coh[index, part, :, here] = coh_in[index, part, :, spans[order]].astype(jnp.float32)
                totals = tuple(
                    advance(index, group, member, order, totals[order]) for order in range(tiles)
                )
            return totals

        totals = lax.fori_loop(0, n_dir // GROUP, step, ((zero, zero),) * tiles)
        return [left_over(order, totals[order]) for order in range(tiles)]

    def project_tile(order):
        def step(group, totals):
            for member in range(GROUP):
                totals = advance(group * GROUP + member, group, member, order, totals)
            return totals

        return left_over(order, lax.fori_loop(0, n_dir // GROUP, step, (zero, zero)))

    def reduce(orders, residuals, opening, closing):
        def step(index, carry):
            if opening:
                total_re, total_im, total_weight = zero, zero, zero
            else:
                total_re, total_im, total_weight = sums[index, 0], sums[index, 1], sums[index, 2]
            for order, (residual_re, residual_im) in zip(orders, residuals):
                here = pl.ds(order * width, width)
                along_re = along[index, 0, :, here]
                along_im = along[index, 1, :, here]
                total_weight += along_re * along_re + along_im * along_im
                total_re += residual_re * along_re + residual_im * along_im
                total_im += residual_im * along_re - residual_re * along_im
            if not closing:
                sums[index, 0] = total_re
                sums[index, 1] = total_im
                sums[index, 2] = total_weight
                return carry
            numer, weights = carry
            sum_re = jnp.sum(total_re, axis=1, keepdims=True)
            sum_im = jnp.sum(total_im, axis=1, keepdims=True)
            sum_weight = jnp.sum(total_weight, axis=1, keepdims=True)
            numer = jnp.where(part_lane == index, sum_re, jnp.where(part_lane == PART + index, sum_im, numer))
            weights = jnp.where(dir_lane == index, sum_weight, weights)
            return numer, weights

        return lax.fori_loop(0, n_dir, step, (zero, zero), unroll=GROUP)

    target = gains
    duals = zero
    for sweep in range(SWEEPS):
        if sweep == 0:
            for order in range(tiles):
                receive_tile(0, order)
            numer, weights = reduce(range(tiles), project_first(), True, True)
        else:
            for order in range(tiles):
                receive_tile(sweep, order)
                residual = project_tile(order)
                numer, weights = reduce([order], [residual], order == 0, order == tiles - 1)
        solved = (numer + gains * weights + strength * (target - duals)) / (weights + strength)
        gains = gains + DAMPING * (solved - gains)
        send_gains(sweep + 1, gains)
        send_mixed(sweep, gains + duals)
        widen(gains)
        if sweep == SWEEPS - 1:
            for part in range(2):
                gains_ref[0, part] = gains[:, part * PART : part * PART + n_dir]
        coefficients = receive_mixed(sweep)
        target = coefficients[0] + own_place * coefficients[1] + own_place * own_place * coefficients[2]
        duals = duals + gains - target
    for order in range(3):
        for part in range(2):
            coeff_ref[order, part] = coefficients[order][:, part * PART : part * PART + n_dir]
    for order in range(tiles):
        receive_tile(SWEEPS, order)
        residual = project_tile(order)
        for part in range(2):
            resid_ref[0, part, :, spans[order]] = residual[part]

    whole = coh_out.at[pl.ds(0, n_dir - 1)]
    pltpu.make_async_copy(whole, whole, coh_send).wait()
    for slot in range(SWEEPS + 1):
        for slab in range(SLABS):
            whole = gain_in.at[slot, slab, pl.ds(0, per_slab - 1 if slab == 0 else per_slab)]
            pltpu.make_async_copy(whole, whole, gain_send.at[slot]).wait()
    for slot in range(SWEEPS):
        whole = mixed_in.at[slot, pl.ds(0, n_band - 1)]
        pltpu.make_async_copy(whole, whole, mixed_send.at[slot]).wait()


def on_device(n_band, n_dir, responses, fluxes, counts, penalty, visibilities, start_gains):
    stations, sources = responses.shape[3], responses.shape[4]
    own = stations // n_dir
    width = stations // SLABS
    per_slab = n_dir // SLABS
    hbm = pl.BlockSpec(memory_space=pltpu.HBM)
    vmem = pl.BlockSpec(memory_space=pltpu.VMEM)
    smem = pl.BlockSpec(memory_space=pltpu.SMEM)
    bf16, f32 = jnp.bfloat16, jnp.float32
    gains, coefficients, residual = pl.pallas_call(
        functools.partial(calibrate, n_band, n_dir),
        out_shape=(
            jax.ShapeDtypeStruct((1, 2, own, n_dir), f32),
            jax.ShapeDtypeStruct((3, 2, own, n_dir), f32),
            jax.ShapeDtypeStruct((1, 2, own, stations), f32),
        ),
        in_specs=[hbm, hbm, smem, smem, hbm, hbm],
        out_specs=(vmem, vmem, vmem),
        scratch_shapes=[
            pltpu.VMEM((2, stations, sources), bf16),
            pltpu.VMEM((1, sources), f32),
            pltpu.VMEM((2, own, stations), f32),
            pltpu.VMEM((2, own, n_dir), f32),
            pltpu.VMEM((2 * stations, sources), bf16),
            pltpu.VMEM((n_dir, 2, own, stations), bf16),
            pltpu.VMEM((n_dir, 2, own, stations), bf16),
            pltpu.VMEM((n_dir, 2, own, stations), f32),
            pltpu.VMEM((n_dir, 2, own, stations), f32),
            pltpu.VMEM((SLABS, 2 * PART // GROUP, GROUP, width), f32),
            pltpu.VMEM((2 * PART, own, 128), f32),
            pltpu.VMEM((n_dir, 3, own, 128), f32),
            pltpu.VMEM((SWEEPS + 1, own, 128), bf16),
            pltpu.VMEM((SWEEPS + 1, SLABS, per_slab, own, 128), bf16),
            pltpu.VMEM((SWEEPS, own, 128), bf16),
            pltpu.VMEM((SWEEPS, n_band, own, 128), bf16),
            pltpu.SemaphoreType.DMA((4,)),
            pltpu.SemaphoreType.DMA,
            pltpu.SemaphoreType.DMA((n_dir,)),
            pltpu.SemaphoreType.DMA((SWEEPS + 1,)),
            pltpu.SemaphoreType.DMA((SWEEPS + 1, SLABS)),
            pltpu.SemaphoreType.DMA((SWEEPS,)),
            pltpu.SemaphoreType.DMA((SWEEPS,)),
        ],
        compiler_params=pltpu.CompilerParams(
            collective_id=0, has_side_effects=True, vmem_limit_bytes=40 * 1024 * 1024
        ),
    )(
        *[pltpu.with_memory_space_constraint(value, pltpu.HBM) for value in (responses, fluxes)],
        counts,
        pltpu.with_memory_space_constraint(penalty, pltpu.HBM),
        pltpu.with_memory_space_constraint(visibilities, pltpu.HBM),
        pltpu.with_memory_space_constraint(jnp.transpose(start_gains, (0, 1, 3, 2)), pltpu.HBM),
    )
    return jnp.transpose(gains, (0, 1, 3, 2)), jnp.transpose(coefficients, (0, 1, 3, 2)), residual


def solution(mesh):
    in_specs = (
        P("band", "dir", None, None, None),
        P("band", "dir", None),
        P("dir"),
        P(),
        P("band", None, "dir", None),
        P("band", None, None, "dir"),
    )
    out_specs = (
        P("band", None, None, "dir"),
        P(None, None, None, "dir"),
        P("band", None, "dir", None),
    )
    return jax.shard_map(
        functools.partial(on_device, mesh.shape["band"], mesh.shape["dir"]),
        mesh=mesh,
        in_specs=in_specs,
        out_specs=out_specs,
        check_vma=False,
    )
```

```python
import functools

import jax
import jax.numpy as jnp
from jax import lax
from jax.experimental import pallas as pl
from jax.experimental.pallas import tpu as pltpu
from jax.sharding import PartitionSpec as P

MESH = pl.DeviceIdType.MESH
SWEEPS = 3
RIDGE_WEIGHT = 0.25
DAMPING = 0.5
SLABS = 4
PART = 32
GROUP = 8
NT = (((1,), (1,)), ((), ()))


def gram_inverse(band_total):
    locations = [(2.0 * position + 1.0 - band_total) / band_total for position in range(band_total)]
    gram = [
        [
            sum((location ** (first + second) for location in locations))
            + (RIDGE_WEIGHT if first == second else 0.0)
            for second in range(3)
        ]
        for first in range(3)
    ]

    def cofactor(first, second):
        rows = [index for index in range(3) if index != first]
        cols = [index for index in range(3) if index != second]
        minor = gram[rows[0]][cols[0]] * gram[rows[1]][cols[1]] - gram[rows[0]][cols[1]] * gram[rows[1]][cols[0]]
        return minor if (first + second) % 2 == 0 else -minor

    determinant = sum((gram[0][column] * cofactor(0, column) for column in range(3)))
    return [[cofactor(column, row) / determinant for column in range(3)] for row in range(3)]


def calibrate(
    n_band,
    n_dir,
    resp_hbm,
    flux_hbm,
    count_ref,
    penalty_ref,
    vis_hbm,
    start_hbm,
    gains_ref,
    coeff_ref,
    resid_ref,
    resp,
    flux,
    vis,
    start,
    scaled,
    coh_out,
    coh_in,
    coh,
    along,
    columns,
    rows_wide,
    sums,
    gain_out,
    gain_in,
    mixed_out,
    mixed_in,
    load_sem,
    coh_send,
    coh_recv,
    gain_send,
    gain_recv,
    start_recv,
    mixed_send,
    mixed_recv,
):
    me = lax.axis_index("dir")
    band = lax.axis_index("band")
    stations, sources = resp.shape[1], resp.shape[2]
    per_slab = n_dir // SLABS
    own = stations // n_dir
    tiles = SLABS
    width = stations // SLABS
    my_slab = me // per_slab
    my_place = lax.rem(me, per_slab)

    loads = [
        pltpu.make_async_copy(source, goal, load_sem.at[index])
        for index, (source, goal) in enumerate(
            (
                (start_hbm.at[0], start),
                (flux_hbm.at[0], flux),
                (vis_hbm.at[0], vis),
            )
        )
    ]
    slabs = [lax.rem(my_slab + offset, SLABS) for offset in (2, 1, 3, 0)]
    for index, slab in enumerate(slabs):
        rows = pl.ds(pl.multiple_of(slab * width, width), width)
        loads.append(
            pltpu.make_async_copy(resp_hbm.at[0, 0, :, rows], resp.at[:, rows], load_sem.at[3 + index])
        )
    for load in loads:
        load.start()

    barrier = pltpu.get_barrier_semaphore()

    rotations = [step for step in (4, 5, 2, 3, 6, 7, 1, 0) if step < per_slab]
    places = [my_place if step == 0 else lax.rem(my_place + step, per_slab) for step in rotations]
    peers = []
    for offset in (2, 1, 3, 0):
        slab = lax.rem(my_slab + offset, SLABS)
        for step, place in zip(rotations, places):
            if offset or step:
                peers.append(slab * per_slab + place)
    bands = [lax.rem(band + step, n_band) for step in range(1, n_band)]
    for peer in peers:
        pl.semaphore_signal(barrier, inc=1, device_id=(band, peer), device_id_type=MESH)
    for peer in bands:
        pl.semaphore_signal(barrier, inc=1, device_id=(peer, me), device_id_type=MESH)

    lane = lax.broadcasted_iota(jnp.int32, (own, 128), 1)
    dir_lane = lane % PART
    part_lane = lane % (2 * PART)
    low_half = lane < 2 * PART
    fold = (
        lax.broadcasted_iota(jnp.int32, (2 * PART, 128), 0)
        == lax.broadcasted_iota(jnp.int32, (2 * PART, 128), 1) % (2 * PART)
    ).astype(jnp.bfloat16)
    zero = jnp.zeros((own, 128), jnp.float32)

    def split(value):
        high = value.astype(jnp.bfloat16).astype(jnp.float32)
        return jnp.where(low_half, high, value - high).astype(jnp.bfloat16)

    strength = jnp.ones((own, 128), jnp.float32)
    for index in range(n_dir):
        strength = jnp.where(dir_lane == index, penalty_ref[index], strength)

    loads[0].wait()
    pieces = []
    for part in range(2):
        pieces.append(start[part])
        if n_dir < PART:
            pieces.append(jnp.zeros((own, PART - n_dir), jnp.float32))
    gains = jnp.concatenate(pieces + pieces, axis=1)

    near = [lax.rem(my_slab + offset, SLABS) for offset in (0, 1, 3, 2)]
    spans = [pl.ds(pl.multiple_of(slab * width, width), width) for slab in near]

    def widen(value):
        for part in range(2):
            for index in range(n_dir):
                place = part * PART + index
                rows_wide[place] = jnp.broadcast_to(value[:, place : place + 1], (own, 128))

    def send_gains(slot, value):
        gain_out[slot] = split(value)
        gain_in[slot, my_slab, my_place] = gain_out[slot]

        for peer in peers:
            pltpu.make_async_remote_copy(
                src_ref=gain_out.at[slot],
                dst_ref=gain_in.at[slot, my_slab, my_place],
                send_sem=gain_send.at[slot],
                recv_sem=gain_recv.at[slot, my_slab],
                device_id=(band, peer),
                device_id_type=MESH,
            ).start()

    def send_start():
        gain_out[0] = split(gains)
        gain_in[0, my_slab, my_place] = gain_out[0]
        for offset in (2, 1, 3):
            pltpu.make_async_remote_copy(
                src_ref=gain_out.at[0],
                dst_ref=gain_in.at[0, my_slab, my_place],
                send_sem=gain_send.at[0],
                recv_sem=start_recv,
                device_id=(band, lax.rem(my_slab + offset, SLABS) * per_slab + my_place),
                device_id_type=MESH,
            ).start()

    def forward_start():
        whole = gain_in.at[0, pl.ds(0, SLABS - 1), 0]
        pltpu.make_async_copy(whole, whole, start_recv).wait()
        for place in places:
            if place is not my_place:
                pltpu.make_async_remote_copy(
                    src_ref=gain_in.at[0, :, my_place],
                    dst_ref=gain_in.at[0, :, my_place],
                    send_sem=gain_send.at[0],
                    recv_sem=gain_recv.at[0, 0],
                    device_id=(band, my_slab * per_slab + place),
                    device_id_type=MESH,
                ).start()

    def receive_start():
        whole = gain_in.at[0, :, pl.ds(0, per_slab - 1)]
        pltpu.make_async_copy(whole, whole, gain_recv.at[0, 0]).wait()
        for order in range(tiles):
            unpack_tile(0, order)

    def receive_tile(slot, order):
        slab = near[order]
        whole = gain_in.at[slot, slab, pl.ds(0, per_slab - 1 if order == 0 else per_slab)]
        pltpu.make_async_copy(whole, whole, gain_recv.at[slot, slab]).wait()
        unpack_tile(slot, order)

    def unpack_tile(slot, order):
        slab = near[order]
        packed = gain_in[slot, slab].reshape(width, 128)
        value = lax.dot_general(fold, packed, NT, preferred_element_type=jnp.float32)
        columns[order] = value.reshape(columns.shape[1:])

    def send_mixed(slot, value):
        mixed_out[slot] = split(value)
        mixed_in[slot, band] = mixed_out[slot]

        for peer in bands:
            pltpu.make_async_remote_copy(
                src_ref=mixed_out.at[slot],
                dst_ref=mixed_in.at[slot, band],
                send_sem=mixed_send.at[slot],
                recv_sem=mixed_recv.at[slot],
                device_id=(peer, me),
                device_id_type=MESH,
            ).start()

    inverse = gram_inverse(n_band)
    own_place = (2.0 * band.astype(jnp.float32) + 1.0 - n_band) / n_band

    def receive_mixed(slot):
        whole = mixed_in.at[slot, pl.ds(0, n_band - 1)]
        pltpu.make_async_copy(whole, whole, mixed_recv.at[slot]).wait()
        totals = [None, None, None]
        for index in range(n_band):
            place = (2.0 * index + 1.0 - n_band) / n_band
            value = mixed_in[slot, index].astype(jnp.float32)
            for order in range(3):
                term = value * (place**order)
                totals[order] = term if totals[order] is None else totals[order] + term
        moments = [value + pltpu.roll(value, 2 * PART, 1) for value in totals]
        return [
            moments[0] * inverse[row][0] + moments[1] * inverse[row][1] + moments[2] * inverse[row][2]
            for row in range(3)
        ]

    loads[1].wait()
    live = lax.broadcasted_iota(jnp.int32, (1, sources), 1) < count_ref[0]
    weight = jnp.where(live, flux[...], 0.0)

    def combine(by_re, by_im, begin_row, begin_col):
        count = by_re.shape[1]
        real = by_re[:width] + by_im[width:]
        imag = by_re[width:] - by_im[:width]
        off = (lax.broadcasted_iota(jnp.int32, (width, count), 0) + begin_row) != (
            lax.broadcasted_iota(jnp.int32, (width, count), 1) + begin_col
        )
        shape = (per_slab, own, count)
        return [jnp.where(off, value, 0.0).astype(jnp.bfloat16).reshape(shape) for value in (real, imag)]

    def left_rows(begin):
        return jnp.concatenate([resp[0, pl.ds(begin, width), :], resp[1, pl.ds(begin, width), :]], axis=0)

    def send_rows(first_dir):
        def send(place, inner):
            peer = first_dir + lax.rem(my_place + per_slab // 2 + place, per_slab)

            @pl.when(peer != me)
            def _():
                pltpu.make_async_remote_copy(
                    src_ref=coh_out.at[peer],
                    dst_ref=coh_in.at[me],
                    send_sem=coh_send,
                    recv_sem=coh_recv.at[me],
                    device_id=(band, peer),
                    device_id_type=MESH,
                ).start()

            return inner

        lax.fori_loop(0, per_slab, send, 0)

    far_begin = pl.multiple_of(slabs[0] * width, width)
    far_dirs = pl.ds(slabs[0] * per_slab, per_slab)
    for index, slab in enumerate(slabs):
        loads[3 + index].wait()
        begin = pl.multiple_of(slab * width, width)
        here = pl.ds(begin, width)
        pieces = []
        for part in range(2):
            piece = (resp[part, here, :].astype(jnp.float32) * weight).astype(jnp.bfloat16)
            scaled[pl.ds(pl.multiple_of(part * stations + begin, width), width), :] = piece
            pieces.append(piece)
        right = jnp.concatenate(pieces, axis=0)
        product = lax.dot_general(left_rows(far_begin), right, NT, preferred_element_type=jnp.float32)
        real, imag = combine(product[:, :width], product[:, width:], far_begin, begin)
        coh_out[far_dirs, 0, :, here] = real
        coh_out[far_dirs, 1, :, here] = imag
    pl.semaphore_wait(barrier, n_dir + n_band - 2)
    send_start()
    send_rows(slabs[0] * per_slab)

    def slab_step(step, carry):
        slab = lax.rem(my_slab + 2 + 3 * step + 3 * (step // 2) + 2 * (step // 3), SLABS)
        begin = pl.multiple_of(slab * width, width)
        left = left_rows(begin)
        by_re = lax.dot_general(left, scaled[:stations], NT, preferred_element_type=jnp.float32)
        by_im = lax.dot_general(left, scaled[stations:], NT, preferred_element_type=jnp.float32)
        first_dir = slab * per_slab
        real, imag = combine(by_re, by_im, begin, 0)
        coh_out[pl.ds(first_dir, per_slab), 0] = real
        coh_out[pl.ds(first_dir, per_slab), 1] = imag
        send_rows(first_dir)
        return carry

    lax.fori_loop(1, SLABS, slab_step, 0)
    coh_in[me] = coh_out[me]
    widen(gains)
    loads[2].wait()
    row_id = lax.broadcasted_iota(jnp.int32, (own, stations), 0) + me * own
    col_id = lax.broadcasted_iota(jnp.int32, (own, stations), 1)
    for part in range(2):
        vis[part] = jnp.where(row_id == col_id, 0.0, vis[part])
    forward_start()

    def advance(index, group, member, order, totals):
        here = pl.ds(order * width, width)
        coh_re = coh[index, 0, :, here]
        coh_im = coh[index, 1, :, here]
        col_re = columns[order, group, member : member + 1]
        col_im = columns[order, PART // GROUP + group, member : member + 1]
        row_re = rows_wide[index]
        row_im = rows_wide[PART + index]
        along_re = coh_re * col_re + coh_im * col_im
        along_im = coh_im * col_re - coh_re * col_im
        along[index, 0, :, here] = along_re
        along[index, 1, :, here] = along_im
        return (
            totals[0] + (row_re * along_re - row_im * along_im),
            totals[1] + (row_re * along_im + row_im * along_re),
        )

    def left_over(order, totals):
        return vis[0, :, spans[order]] - totals[0], vis[1, :, spans[order]] - totals[1]

    def project_first():
        groups = n_dir // GROUP

        def step(turn, totals):
            group = lax.rem(me // GROUP + turn + turn // 2 - 2 * (turn // 3), groups)
            for member in range(GROUP):
                index = group * GROUP + member

                @pl.when(index != me)
                def _(index=index):
                    block = coh_in.at[index]
                    pltpu.make_async_copy(block, block, coh_recv.at[index]).wait()

                for order in range(tiles):
                    here = pl.ds(order * width, width)
                    for part in range(2):
                        coh[index, part, :, here] = coh_in[index, part, :, spans[order]].astype(jnp.float32)
                totals = tuple(
                    advance(index, group, member, order, totals[order]) for order in range(tiles)
                )
            return totals

        totals = lax.fori_loop(0, n_dir // GROUP, step, ((zero, zero),) * tiles)
        return [left_over(order, totals[order]) for order in range(tiles)]

    def project_tile(order):
        def step(group, totals):
            for member in range(GROUP):
                totals = advance(group * GROUP + member, group, member, order, totals)
            return totals

        return left_over(order, lax.fori_loop(0, n_dir // GROUP, step, (zero, zero)))

    def reduce(orders, residuals, opening, closing):
        def step(index, carry):
            if opening:
                total_re, total_im, total_weight = zero, zero, zero
            else:
                total_re, total_im, total_weight = sums[index, 0], sums[index, 1], sums[index, 2]
            for order, (residual_re, residual_im) in zip(orders, residuals):
                here = pl.ds(order * width, width)
                along_re = along[index, 0, :, here]
                along_im = along[index, 1, :, here]
                total_weight += along_re * along_re + along_im * along_im
                total_re += residual_re * along_re + residual_im * along_im
                total_im += residual_im * along_re - residual_re * along_im
            if not closing:
                sums[index, 0] = total_re
                sums[index, 1] = total_im
                sums[index, 2] = total_weight
                return carry
            numer, weights = carry
            sum_re = jnp.sum(total_re, axis=1, keepdims=True)
            sum_im = jnp.sum(total_im, axis=1, keepdims=True)
            sum_weight = jnp.sum(total_weight, axis=1, keepdims=True)
            numer = jnp.where(part_lane == index, sum_re, jnp.where(part_lane == PART + index, sum_im, numer))
            weights = jnp.where(dir_lane == index, sum_weight, weights)
            return numer, weights

        return lax.fori_loop(0, n_dir, step, (zero, zero), unroll=GROUP)

    def agree(slot, value, duals):
        coefficients = receive_mixed(slot)
        target = coefficients[0] + own_place * coefficients[1] + own_place * own_place * coefficients[2]
        return target, duals + value - target

    target = gains
    duals = zero
    for sweep in range(SWEEPS):
        if sweep == 0:
            receive_start()
            numer, weights = reduce(range(tiles), project_first(), True, True)
        else:
            for order in range(tiles):
                if order == tiles - 1:
                    target, duals = agree(sweep - 1, gains, duals)
                receive_tile(sweep, order)
                residual = project_tile(order)
                numer, weights = reduce([order], [residual], order == 0, order == tiles - 1)
        solved = (numer + gains * weights + strength * (target - duals)) / (weights + strength)
        gains = gains + DAMPING * (solved - gains)
        send_gains(sweep + 1, gains)
        send_mixed(sweep, gains + duals)
        widen(gains)
        if sweep == SWEEPS - 1:
            for part in range(2):
                gains_ref[0, part] = gains[:, part * PART : part * PART + n_dir]
    for order in range(tiles):
        if order == tiles - 1:
            coefficients = receive_mixed(SWEEPS - 1)
            for index in range(3):
                for part in range(2):
                    coeff_ref[index, part] = coefficients[index][:, part * PART : part * PART + n_dir]
        receive_tile(SWEEPS, order)
        residual = project_tile(order)
        for part in range(2):
            resid_ref[0, part, :, spans[order]] = residual[part]

    whole = coh_out.at[pl.ds(0, n_dir - 1)]
    pltpu.make_async_copy(whole, whole, coh_send).wait()
    for slot in range(SWEEPS + 1):
        for slab in range(SLABS):
            whole = gain_in.at[slot, slab, pl.ds(0, per_slab - 1 if slab == 0 else per_slab)]
            pltpu.make_async_copy(whole, whole, gain_send.at[slot]).wait()
    for slot in range(SWEEPS):
        whole = mixed_in.at[slot, pl.ds(0, n_band - 1)]
        pltpu.make_async_copy(whole, whole, mixed_send.at[slot]).wait()


def on_device(n_band, n_dir, responses, fluxes, counts, penalty, visibilities, start_gains):
    stations, sources = responses.shape[3], responses.shape[4]
    own = stations // n_dir
    width = stations // SLABS
    per_slab = n_dir // SLABS
    hbm = pl.BlockSpec(memory_space=pltpu.HBM)
    vmem = pl.BlockSpec(memory_space=pltpu.VMEM)
    smem = pl.BlockSpec(memory_space=pltpu.SMEM)
    bf16, f32 = jnp.bfloat16, jnp.float32
    gains, coefficients, residual = pl.pallas_call(
        functools.partial(calibrate, n_band, n_dir),
        out_shape=(
            jax.ShapeDtypeStruct((1, 2, own, n_dir), f32),
            jax.ShapeDtypeStruct((3, 2, own, n_dir), f32),
            jax.ShapeDtypeStruct((1, 2, own, stations), f32),
        ),
        in_specs=[hbm, hbm, smem, smem, hbm, hbm],
        out_specs=(vmem, vmem, vmem),
        scratch_shapes=[
            pltpu.VMEM((2, stations, sources), bf16),
            pltpu.VMEM((1, sources), f32),
            pltpu.VMEM((2, own, stations), f32),
            pltpu.VMEM((2, own, n_dir), f32),
            pltpu.VMEM((2 * stations, sources), bf16),
            pltpu.VMEM((n_dir, 2, own, stations), bf16),
            pltpu.VMEM((n_dir, 2, own, stations), bf16),
            pltpu.VMEM((n_dir, 2, own, stations), f32),
            pltpu.VMEM((n_dir, 2, own, stations), f32),
            pltpu.VMEM((SLABS, 2 * PART // GROUP, GROUP, width), f32),
            pltpu.VMEM((2 * PART, own, 128), f32),
            pltpu.VMEM((n_dir, 3, own, 128), f32),
            pltpu.VMEM((SWEEPS + 1, own, 128), bf16),
            pltpu.VMEM((SWEEPS + 1, SLABS, per_slab, own, 128), bf16),
            pltpu.VMEM((SWEEPS, own, 128), bf16),
            pltpu.VMEM((SWEEPS, n_band, own, 128), bf16),
            pltpu.SemaphoreType.DMA((3 + SLABS,)),
            pltpu.SemaphoreType.DMA,
            pltpu.SemaphoreType.DMA((n_dir,)),
            pltpu.SemaphoreType.DMA((SWEEPS + 1,)),
            pltpu.SemaphoreType.DMA((SWEEPS + 1, SLABS)),
            pltpu.SemaphoreType.DMA,
            pltpu.SemaphoreType.DMA((SWEEPS,)),
            pltpu.SemaphoreType.DMA((SWEEPS,)),
        ],
        compiler_params=pltpu.CompilerParams(
            collective_id=0, has_side_effects=True, vmem_limit_bytes=40 * 1024 * 1024
        ),
    )(
        *[pltpu.with_memory_space_constraint(value, pltpu.HBM) for value in (responses, fluxes)],
        counts,
        pltpu.with_memory_space_constraint(penalty, pltpu.HBM),
        pltpu.with_memory_space_constraint(visibilities, pltpu.HBM),
        pltpu.with_memory_space_constraint(jnp.transpose(start_gains, (0, 1, 3, 2)), pltpu.HBM),
    )
    return jnp.transpose(gains, (0, 1, 3, 2)), jnp.transpose(coefficients, (0, 1, 3, 2)), residual


def solution(mesh):
    in_specs = (
        P("band", "dir", None, None, None),
        P("band", "dir", None),
        P("dir"),
        P(),
        P("band", None, "dir", None),
        P("band", None, None, "dir"),
    )
    out_specs = (
        P("band", None, None, "dir"),
        P(None, None, None, "dir"),
        P("band", None, "dir", None),
    )
    return jax.shard_map(
        functools.partial(on_device, mesh.shape["band"], mesh.shape["dir"]),
        mesh=mesh,
        in_specs=in_specs,
        out_specs=out_specs,
        check_vma=False,
    )
```

```python
import functools

import jax
import jax.numpy as jnp
from jax import lax
from jax.experimental import pallas as pl
from jax.experimental.pallas import tpu as pltpu
from jax.sharding import PartitionSpec as P

MESH = pl.DeviceIdType.MESH
SWEEPS = 3
RIDGE_WEIGHT = 0.25
DAMPING = 0.5
SLABS = 4
PART = 32
GROUP = 8
NT = (((1,), (1,)), ((), ()))


def gram_inverse(band_total):
    locations = [(2.0 * position + 1.0 - band_total) / band_total for position in range(band_total)]
    gram = [
        [
            sum((location ** (first + second) for location in locations))
            + (RIDGE_WEIGHT if first == second else 0.0)
            for second in range(3)
        ]
        for first in range(3)
    ]

    def cofactor(first, second):
        rows = [index for index in range(3) if index != first]
        cols = [index for index in range(3) if index != second]
        minor = gram[rows[0]][cols[0]] * gram[rows[1]][cols[1]] - gram[rows[0]][cols[1]] * gram[rows[1]][cols[0]]
        return minor if (first + second) % 2 == 0 else -minor

    determinant = sum((gram[0][column] * cofactor(0, column) for column in range(3)))
    return [[cofactor(column, row) / determinant for column in range(3)] for row in range(3)]


def calibrate(
    n_band,
    n_dir,
    resp_hbm,
    flux_hbm,
    count_hbm,
    penalty_hbm,
    vis_hbm,
    start_hbm,
    gains_ref,
    coeff_ref,
    resid_ref,
    resp,
    flux,
    vis,
    start,
    count,
    penalty,
    scaled,
    coh_out,
    coh_in,
    coh,
    along,
    columns,
    rows_wide,
    sums,
    gain_out,
    gain_in,
    mixed_out,
    mixed_in,
    load_sem,
    coh_send,
    coh_recv,
    gain_send,
    gain_recv,
    start_recv,
    mixed_send,
    mixed_recv,
):
    me = lax.axis_index("dir")
    band = lax.axis_index("band")
    stations, sources = resp.shape[1], resp.shape[2]
    per_slab = n_dir // SLABS
    own = stations // n_dir
    tiles = SLABS
    width = stations // SLABS
    my_slab = me // per_slab
    my_place = lax.rem(me, per_slab)

    slabs = [lax.rem(my_slab + offset, SLABS) for offset in (2, 1, 3, 0)]
    chunks = [pl.ds(pl.multiple_of(slab * width, width), width) for slab in slabs]
    small = [
        pltpu.make_async_copy(source, goal, load_sem.at[SLABS + index])
        for index, (source, goal) in enumerate(
            (
                (flux_hbm.at[0], flux),
                (count_hbm, count),
                (start_hbm.at[0], start),
                (penalty_hbm, penalty),
                (vis_hbm.at[0], vis),
            )
        )
    ]
    large = [
        pltpu.make_async_copy(resp_hbm.at[0, 0, :, rows], resp.at[:, rows], load_sem.at[index])
        for index, rows in enumerate(chunks)
    ]
    for load in small[:2] + large + small[2:]:
        load.start()

    barrier = pltpu.get_barrier_semaphore()

    rotations = [step for step in (4, 5, 2, 3, 6, 7, 1, 0) if step < per_slab]
    places = [my_place if step == 0 else lax.rem(my_place + step, per_slab) for step in rotations]
    peers = []
    for offset in (2, 1, 3, 0):
        slab = lax.rem(my_slab + offset, SLABS)
        for step, place in zip(rotations, places):
            if offset or step:
                peers.append(slab * per_slab + place)
    bands = [lax.rem(band + step, n_band) for step in range(1, n_band)]
    for peer in peers:
        pl.semaphore_signal(barrier, inc=1, device_id=(band, peer), device_id_type=MESH)
    for peer in bands:
        pl.semaphore_signal(barrier, inc=1, device_id=(peer, me), device_id_type=MESH)

    lane = lax.broadcasted_iota(jnp.int32, (own, 128), 1)
    dir_lane = lane % PART
    part_lane = lane % (2 * PART)
    low_half = lane < 2 * PART
    fold = (
        lax.broadcasted_iota(jnp.int32, (2 * PART, 128), 0)
        == lax.broadcasted_iota(jnp.int32, (2 * PART, 128), 1) % (2 * PART)
    ).astype(jnp.bfloat16)
    zero = jnp.zeros((own, 128), jnp.float32)

    def split(value):
        high = value.astype(jnp.bfloat16).astype(jnp.float32)
        return jnp.where(low_half, high, value - high).astype(jnp.bfloat16)

    near = [lax.rem(my_slab + offset, SLABS) for offset in (0, 1, 3, 2)]
    spans = [pl.ds(pl.multiple_of(slab * width, width), width) for slab in near]

    def widen(value):
        for part in range(2):
            for index in range(n_dir):
                place = part * PART + index
                rows_wide[place] = jnp.broadcast_to(value[:, place : place + 1], (own, 128))

    def send_gains(slot, value):
        gain_out[slot] = split(value)
        gain_in[slot, my_slab, my_place] = gain_out[slot]

        for peer in peers:
            pltpu.make_async_remote_copy(
                src_ref=gain_out.at[slot],
                dst_ref=gain_in.at[slot, my_slab, my_place],
                send_sem=gain_send.at[slot],
                recv_sem=gain_recv.at[slot, my_slab],
                device_id=(band, peer),
                device_id_type=MESH,
            ).start()

    def send_start(gains):
        gain_out[0] = split(gains)
        gain_in[0, my_slab, my_place] = gain_out[0]
        for offset in (2, 1, 3):
            pltpu.make_async_remote_copy(
                src_ref=gain_out.at[0],
                dst_ref=gain_in.at[0, my_slab, my_place],
                send_sem=gain_send.at[0],
                recv_sem=start_recv,
                device_id=(band, lax.rem(my_slab + offset, SLABS) * per_slab + my_place),
                device_id_type=MESH,
            ).start()

    def forward_start():
        whole = gain_in.at[0, pl.ds(0, SLABS - 1), 0]
        pltpu.make_async_copy(whole, whole, start_recv).wait()
        for place in places:
            if place is not my_place:
                pltpu.make_async_remote_copy(
                    src_ref=gain_in.at[0, :, my_place],
                    dst_ref=gain_in.at[0, :, my_place],
                    send_sem=gain_send.at[0],
                    recv_sem=gain_recv.at[0, 0],
                    device_id=(band, my_slab * per_slab + place),
                    device_id_type=MESH,
                ).start()

    def receive_start():
        whole = gain_in.at[0, :, pl.ds(0, per_slab - 1)]
        pltpu.make_async_copy(whole, whole, gain_recv.at[0, 0]).wait()
        for order in range(tiles):
            unpack_tile(0, order)

    def receive_tile(slot, order):
        slab = near[order]
        whole = gain_in.at[slot, slab, pl.ds(0, per_slab - 1 if order == 0 else per_slab)]
        pltpu.make_async_copy(whole, whole, gain_recv.at[slot, slab]).wait()
        unpack_tile(slot, order)

    def unpack_tile(slot, order):
        slab = near[order]
        packed = gain_in[slot, slab].reshape(width, 128)
        value = lax.dot_general(fold, packed, NT, preferred_element_type=jnp.float32)
        columns[order] = value.reshape(columns.shape[1:])

    def send_mixed(slot, value):
        mixed_out[slot] = split(value)
        mixed_in[slot, band] = mixed_out[slot]

        for peer in bands:
            pltpu.make_async_remote_copy(
                src_ref=mixed_out.at[slot],
                dst_ref=mixed_in.at[slot, band],
                send_sem=mixed_send.at[slot],
                recv_sem=mixed_recv.at[slot],
                device_id=(peer, me),
                device_id_type=MESH,
            ).start()

    inverse = gram_inverse(n_band)
    own_place = (2.0 * band.astype(jnp.float32) + 1.0 - n_band) / n_band

    def receive_mixed(slot):
        whole = mixed_in.at[slot, pl.ds(0, n_band - 1)]
        pltpu.make_async_copy(whole, whole, mixed_recv.at[slot]).wait()
        totals = [None, None, None]
        for index in range(n_band):
            place = (2.0 * index + 1.0 - n_band) / n_band
            value = mixed_in[slot, index].astype(jnp.float32)
            for order in range(3):
                term = value * (place**order)
                totals[order] = term if totals[order] is None else totals[order] + term
        moments = [value + pltpu.roll(value, 2 * PART, 1) for value in totals]
        return [
            moments[0] * inverse[row][0] + moments[1] * inverse[row][1] + moments[2] * inverse[row][2]
            for row in range(3)
        ]

    small[0].wait()
    small[1].wait()
    live = lax.broadcasted_iota(jnp.int32, (1, sources), 1) < count[0]
    weight = jnp.where(live, flux[...], 0.0)

    def combine(by_re, by_im, begin_row, begin_col):
        count = by_re.shape[1]
        real = by_re[:width] + by_im[width:]
        imag = by_re[width:] - by_im[:width]
        off = (lax.broadcasted_iota(jnp.int32, (width, count), 0) + begin_row) != (
            lax.broadcasted_iota(jnp.int32, (width, count), 1) + begin_col
        )
        shape = (per_slab, own, count)
        return [jnp.where(off, value, 0.0).astype(jnp.bfloat16).reshape(shape) for value in (real, imag)]

    def left_rows(begin):
        return jnp.concatenate([resp[0, pl.ds(begin, width), :], resp[1, pl.ds(begin, width), :]], axis=0)

    def send_rows(first_dir):
        def send(place, inner):
            peer = first_dir + lax.rem(my_place + per_slab // 2 + place, per_slab)

            @pl.when(peer != me)
            def _():
                pltpu.make_async_remote_copy(
                    src_ref=coh_out.at[peer],
                    dst_ref=coh_in.at[me],
                    send_sem=coh_send,
                    recv_sem=coh_recv.at[me],
                    device_id=(band, peer),
                    device_id_type=MESH,
                ).start()

            return inner

        lax.fori_loop(0, per_slab, send, 0)

    far_begin = pl.multiple_of(slabs[0] * width, width)
    far_dirs = pl.ds(slabs[0] * per_slab, per_slab)
    for index, slab in enumerate(slabs):
        large[index].wait()
        begin = pl.multiple_of(slab * width, width)
        here = pl.ds(begin, width)
        pieces = []
        for part in range(2):
            piece = (resp[part, here, :].astype(jnp.float32) * weight).astype(jnp.bfloat16)
            scaled[pl.ds(pl.multiple_of(part * stations + begin, width), width), :] = piece
            pieces.append(piece)
        right = jnp.concatenate(pieces, axis=0)
        product = lax.dot_general(left_rows(far_begin), right, NT, preferred_element_type=jnp.float32)
        real, imag = combine(product[:, :width], product[:, width:], far_begin, begin)
        coh_out[far_dirs, 0, :, here] = real
        coh_out[far_dirs, 1, :, here] = imag
    pl.semaphore_wait(barrier, n_dir + n_band - 2)
    small[3].wait()
    strength = jnp.ones((own, 128), jnp.float32)
    for index in range(n_dir):
        strength = jnp.where(dir_lane == index, penalty[index], strength)

    small[2].wait()
    pieces = []
    for part in range(2):
        pieces.append(start[part])
        if n_dir < PART:
            pieces.append(jnp.zeros((own, PART - n_dir), jnp.float32))
    gains = jnp.concatenate(pieces + pieces, axis=1)

    send_start(gains)
    send_rows(slabs[0] * per_slab)

    def slab_step(step, carry):
        slab = lax.rem(my_slab + 2 + 3 * step + 3 * (step // 2) + 2 * (step // 3), SLABS)
        begin = pl.multiple_of(slab * width, width)
        left = left_rows(begin)
        by_re = lax.dot_general(left, scaled[:stations], NT, preferred_element_type=jnp.float32)
        by_im = lax.dot_general(left, scaled[stations:], NT, preferred_element_type=jnp.float32)
        first_dir = slab * per_slab
        real, imag = combine(by_re, by_im, begin, 0)
        coh_out[pl.ds(first_dir, per_slab), 0] = real
        coh_out[pl.ds(first_dir, per_slab), 1] = imag
        send_rows(first_dir)
        return carry

    lax.fori_loop(1, SLABS, slab_step, 0)
    coh_in[me] = coh_out[me]
    widen(gains)
    small[4].wait()
    row_id = lax.broadcasted_iota(jnp.int32, (own, stations), 0) + me * own
    col_id = lax.broadcasted_iota(jnp.int32, (own, stations), 1)
    for part in range(2):
        vis[part] = jnp.where(row_id == col_id, 0.0, vis[part])
    forward_start()

    def advance(index, group, member, order, totals):
        here = pl.ds(order * width, width)
        coh_re = coh[index, 0, :, here]
        coh_im = coh[index, 1, :, here]
        col_re = columns[order, group, member : member + 1]
        col_im = columns[order, PART // GROUP + group, member : member + 1]
        row_re = rows_wide[index]
        row_im = rows_wide[PART + index]
        along_re = coh_re * col_re + coh_im * col_im
        along_im = coh_im * col_re - coh_re * col_im
        along[index, 0, :, here] = along_re
        along[index, 1, :, here] = along_im
        return (
            totals[0] + (row_re * along_re - row_im * along_im),
            totals[1] + (row_re * along_im + row_im * along_re),
        )

    def left_over(order, totals):
        return vis[0, :, spans[order]] - totals[0], vis[1, :, spans[order]] - totals[1]

    def project_first():
        groups = n_dir // GROUP

        def step(turn, totals):
            group = lax.rem(me // GROUP + turn + turn // 2 - 2 * (turn // 3), groups)
            for member in range(GROUP):
                index = group * GROUP + member

                @pl.when(index != me)
                def _(index=index):
                    block = coh_in.at[index]
                    pltpu.make_async_copy(block, block, coh_recv.at[index]).wait()

                for order in range(tiles):
                    here = pl.ds(order * width, width)
                    for part in range(2):
                        coh[index, part, :, here] = coh_in[index, part, :, spans[order]].astype(jnp.float32)
                totals = tuple(
                    advance(index, group, member, order, totals[order]) for order in range(tiles)
                )
            return totals

        totals = lax.fori_loop(0, n_dir // GROUP, step, ((zero, zero),) * tiles)
        return [left_over(order, totals[order]) for order in range(tiles)]

    def project_tile(order):
        def step(group, totals):
            for member in range(GROUP):
                totals = advance(group * GROUP + member, group, member, order, totals)
            return totals

        return left_over(order, lax.fori_loop(0, n_dir // GROUP, step, (zero, zero)))

    def reduce(orders, residuals, opening, closing):
        def step(index, carry):
            if opening:
                total_re, total_im, total_weight = zero, zero, zero
            else:
                total_re, total_im, total_weight = sums[index, 0], sums[index, 1], sums[index, 2]
            for order, (residual_re, residual_im) in zip(orders, residuals):
                here = pl.ds(order * width, width)
                along_re = along[index, 0, :, here]
                along_im = along[index, 1, :, here]
                total_weight += along_re * along_re + along_im * along_im
                total_re += residual_re * along_re + residual_im * along_im
                total_im += residual_im * along_re - residual_re * along_im
            if not closing:
                sums[index, 0] = total_re
                sums[index, 1] = total_im
                sums[index, 2] = total_weight
                return carry
            numer, weights = carry
            sum_re = jnp.sum(total_re, axis=1, keepdims=True)
            sum_im = jnp.sum(total_im, axis=1, keepdims=True)
            sum_weight = jnp.sum(total_weight, axis=1, keepdims=True)
            numer = jnp.where(part_lane == index, sum_re, jnp.where(part_lane == PART + index, sum_im, numer))
            weights = jnp.where(dir_lane == index, sum_weight, weights)
            return numer, weights

        return lax.fori_loop(0, n_dir, step, (zero, zero), unroll=n_dir if closing else GROUP)

    def agree(slot, value, duals):
        coefficients = receive_mixed(slot)
        target = coefficients[0] + own_place * coefficients[1] + own_place * own_place * coefficients[2]
        return target, duals + value - target

    target = gains
    duals = zero
    for sweep in range(SWEEPS):
        if sweep == 0:
            receive_start()
            numer, weights = reduce(range(tiles), project_first(), True, True)
        else:
            for order in range(tiles):
                if order == tiles - 1:
                    target, duals = agree(sweep - 1, gains, duals)
                receive_tile(sweep, order)
                residual = project_tile(order)
                numer, weights = reduce([order], [residual], order == 0, order == tiles - 1)
        solved = (numer + gains * weights + strength * (target - duals)) / (weights + strength)
        gains = gains + DAMPING * (solved - gains)
        send_gains(sweep + 1, gains)
        send_mixed(sweep, gains + duals)
        widen(gains)
        if sweep == SWEEPS - 1:
            for part in range(2):
                gains_ref[0, part] = gains[:, part * PART : part * PART + n_dir]
    for order in range(tiles):
        if order == tiles - 1:
            coefficients = receive_mixed(SWEEPS - 1)
            for index in range(3):
                for part in range(2):
                    coeff_ref[index, part] = coefficients[index][:, part * PART : part * PART + n_dir]
        receive_tile(SWEEPS, order)
        residual = project_tile(order)
        for part in range(2):
            resid_ref[0, part, :, spans[order]] = residual[part]

    whole = coh_out.at[pl.ds(0, n_dir - 1)]
    pltpu.make_async_copy(whole, whole, coh_send).wait()
    for slot in range(SWEEPS + 1):
        for slab in range(SLABS):
            whole = gain_in.at[slot, slab, pl.ds(0, per_slab - 1 if slab == 0 else per_slab)]
            pltpu.make_async_copy(whole, whole, gain_send.at[slot]).wait()
    for slot in range(SWEEPS):
        whole = mixed_in.at[slot, pl.ds(0, n_band - 1)]
        pltpu.make_async_copy(whole, whole, mixed_send.at[slot]).wait()


def on_device(n_band, n_dir, responses, fluxes, counts, penalty, visibilities, start_gains):
    stations, sources = responses.shape[3], responses.shape[4]
    own = stations // n_dir
    width = stations // SLABS
    per_slab = n_dir // SLABS
    hbm = pl.BlockSpec(memory_space=pltpu.HBM)
    vmem = pl.BlockSpec(memory_space=pltpu.VMEM)
    bf16, f32 = jnp.bfloat16, jnp.float32
    gains, coefficients, residual = pl.pallas_call(
        functools.partial(calibrate, n_band, n_dir),
        out_shape=(
            jax.ShapeDtypeStruct((1, 2, own, n_dir), f32),
            jax.ShapeDtypeStruct((3, 2, own, n_dir), f32),
            jax.ShapeDtypeStruct((1, 2, own, stations), f32),
        ),
        in_specs=[hbm] * 6,
        out_specs=(vmem, vmem, vmem),
        scratch_shapes=[
            pltpu.VMEM((2, stations, sources), bf16),
            pltpu.VMEM((1, sources), f32),
            pltpu.VMEM((2, own, stations), f32),
            pltpu.VMEM((2, own, n_dir), f32),
            pltpu.SMEM((1,), jnp.int32),
            pltpu.SMEM((n_dir,), f32),
            pltpu.VMEM((2 * stations, sources), bf16),
            pltpu.VMEM((n_dir, 2, own, stations), bf16),
            pltpu.VMEM((n_dir, 2, own, stations), bf16),
            pltpu.VMEM((n_dir, 2, own, stations), f32),
            pltpu.VMEM((n_dir, 2, own, stations), f32),
            pltpu.VMEM((SLABS, 2 * PART // GROUP, GROUP, width), f32),
            pltpu.VMEM((2 * PART, own, 128), f32),
            pltpu.VMEM((n_dir, 3, own, 128), f32),
            pltpu.VMEM((SWEEPS + 1, own, 128), bf16),
            pltpu.VMEM((SWEEPS + 1, SLABS, per_slab, own, 128), bf16),
            pltpu.VMEM((SWEEPS, own, 128), bf16),
            pltpu.VMEM((SWEEPS, n_band, own, 128), bf16),
            pltpu.SemaphoreType.DMA((SLABS + 5,)),
            pltpu.SemaphoreType.DMA,
            pltpu.SemaphoreType.DMA((n_dir,)),
            pltpu.SemaphoreType.DMA((SWEEPS + 1,)),
            pltpu.SemaphoreType.DMA((SWEEPS + 1, SLABS)),
            pltpu.SemaphoreType.DMA,
            pltpu.SemaphoreType.DMA((SWEEPS,)),
            pltpu.SemaphoreType.DMA((SWEEPS,)),
        ],
        compiler_params=pltpu.CompilerParams(
            collective_id=0, has_side_effects=True, vmem_limit_bytes=40 * 1024 * 1024
        ),
    )(
        *[pltpu.with_memory_space_constraint(value, pltpu.HBM) for value in (responses, fluxes)],
        counts,
        pltpu.with_memory_space_constraint(penalty, pltpu.HBM),
        pltpu.with_memory_space_constraint(visibilities, pltpu.HBM),
        pltpu.with_memory_space_constraint(jnp.transpose(start_gains, (0, 1, 3, 2)), pltpu.HBM),
    )
    return jnp.transpose(gains, (0, 1, 3, 2)), jnp.transpose(coefficients, (0, 1, 3, 2)), residual


def solution(mesh):
    in_specs = (
        P("band", "dir", None, None, None),
        P("band", "dir", None),
        P("dir"),
        P(),
        P("band", None, "dir", None),
        P("band", None, None, "dir"),
    )
    out_specs = (
        P("band", None, None, "dir"),
        P(None, None, None, "dir"),
        P("band", None, "dir", None),
    )
    return jax.shard_map(
        functools.partial(on_device, mesh.shape["band"], mesh.shape["dir"]),
        mesh=mesh,
        in_specs=in_specs,
        out_specs=out_specs,
        check_vma=False,
    )
```

```python
import functools

import jax
import jax.numpy as jnp
from jax import lax
from jax.experimental import pallas as pl
from jax.experimental.pallas import tpu as pltpu
from jax.sharding import PartitionSpec as P

MESH = pl.DeviceIdType.MESH
SWEEPS = 3
RIDGE_WEIGHT = 0.25
DAMPING = 0.5
SLABS = 4
PART = 32
GROUP = 8
NT = (((1,), (1,)), ((), ()))


def gram_inverse(band_total):
    locations = [(2.0 * position + 1.0 - band_total) / band_total for position in range(band_total)]
    gram = [
        [
            sum((location ** (first + second) for location in locations))
            + (RIDGE_WEIGHT if first == second else 0.0)
            for second in range(3)
        ]
        for first in range(3)
    ]

    def cofactor(first, second):
        rows = [index for index in range(3) if index != first]
        cols = [index for index in range(3) if index != second]
        minor = gram[rows[0]][cols[0]] * gram[rows[1]][cols[1]] - gram[rows[0]][cols[1]] * gram[rows[1]][cols[0]]
        return minor if (first + second) % 2 == 0 else -minor

    determinant = sum((gram[0][column] * cofactor(0, column) for column in range(3)))
    return [[cofactor(column, row) / determinant for column in range(3)] for row in range(3)]


def calibrate(
    n_band,
    n_dir,
    resp_hbm,
    flux_hbm,
    count_hbm,
    penalty_hbm,
    vis_hbm,
    start_hbm,
    gains_ref,
    coeff_ref,
    resid_ref,
    resp,
    flux,
    vis,
    start,
    count,
    penalty,
    scaled,
    coh_out,
    coh_in,
    coh,
    along,
    columns,
    rows_wide,
    sums,
    gain_out,
    gain_in,
    mixed_out,
    mixed_in,
    load_sem,
    coh_send,
    coh_recv,
    gain_send,
    gain_recv,
    start_recv,
    mixed_send,
    mixed_recv,
):
    me = lax.axis_index("dir")
    band = lax.axis_index("band")
    stations, sources = resp.shape[1], resp.shape[2]
    per_slab = n_dir // SLABS
    own = stations // n_dir
    tiles = SLABS
    width = stations // SLABS
    my_slab = me // per_slab
    my_place = lax.rem(me, per_slab)

    slabs = [lax.rem(my_slab + offset, SLABS) for offset in (2, 1, 3, 0)]
    chunks = [pl.ds(pl.multiple_of(slab * width, width), width) for slab in slabs]
    small = [
        pltpu.make_async_copy(source, goal, load_sem.at[SLABS + index])
        for index, (source, goal) in enumerate(
            (
                (flux_hbm.at[0], flux),
                (count_hbm, count),
                (start_hbm.at[0], start),
                (penalty_hbm, penalty),
                (vis_hbm.at[0], vis),
            )
        )
    ]
    large = [
        pltpu.make_async_copy(resp_hbm.at[0, 0, :, rows], resp.at[:, rows], load_sem.at[index])
        for index, rows in enumerate(chunks)
    ]
    for load in small[:2] + large + small[2:]:
        load.start()

    barrier = pltpu.get_barrier_semaphore()

    rotations = [step for step in (4, 5, 2, 3, 6, 7, 1, 0) if step < per_slab]
    places = [my_place if step == 0 else lax.rem(my_place + step, per_slab) for step in rotations]
    peers = []
    for offset in (2, 1, 3, 0):
        slab = lax.rem(my_slab + offset, SLABS)
        for step, place in zip(rotations, places):
            if offset or step:
                peers.append(slab * per_slab + place)
    bands = [lax.rem(band + step, n_band) for step in range(1, n_band)]
    for peer in peers:
        pl.semaphore_signal(barrier, inc=1, device_id=(band, peer), device_id_type=MESH)
    for peer in bands:
        pl.semaphore_signal(barrier, inc=1, device_id=(peer, me), device_id_type=MESH)

    lane = lax.broadcasted_iota(jnp.int32, (own, 128), 1)
    dir_lane = lane % PART
    part_lane = lane % (2 * PART)
    low_half = lane < 2 * PART
    fold = (
        lax.broadcasted_iota(jnp.int32, (2 * PART, 128), 0)
        == lax.broadcasted_iota(jnp.int32, (2 * PART, 128), 1) % (2 * PART)
    ).astype(jnp.bfloat16)
    zero = jnp.zeros((own, 128), jnp.float32)

    def split(value):
        high = value.astype(jnp.bfloat16).astype(jnp.float32)
        return jnp.where(low_half, high, value - high).astype(jnp.bfloat16)

    near = [lax.rem(my_slab + offset, SLABS) for offset in (0, 1, 3, 2)]
    spans = [pl.ds(pl.multiple_of(slab * width, width), width) for slab in near]

    def widen(value):
        for part in range(2):
            for index in range(n_dir):
                place = part * PART + index
                rows_wide[place] = jnp.broadcast_to(value[:, place : place + 1], (own, 128))

    def send_gains(slot, value):
        gain_out[slot] = split(value)
        gain_in[slot, my_slab, my_place] = gain_out[slot]

        for peer in peers:
            pltpu.make_async_remote_copy(
                src_ref=gain_out.at[slot],
                dst_ref=gain_in.at[slot, my_slab, my_place],
                send_sem=gain_send.at[slot],
                recv_sem=gain_recv.at[slot, my_slab],
                device_id=(band, peer),
                device_id_type=MESH,
            ).start()

    def send_start(gains):
        gain_out[0] = split(gains)
        gain_in[0, my_slab, my_place] = gain_out[0]
        for offset in (2, 1, 3):
            pltpu.make_async_remote_copy(
                src_ref=gain_out.at[0],
                dst_ref=gain_in.at[0, my_slab, my_place],
                send_sem=gain_send.at[0],
                recv_sem=start_recv,
                device_id=(band, lax.rem(my_slab + offset, SLABS) * per_slab + my_place),
                device_id_type=MESH,
            ).start()

    def forward_start():
        whole = gain_in.at[0, pl.ds(0, SLABS - 1), 0]
        pltpu.make_async_copy(whole, whole, start_recv).wait()
        for place in places:
            if place is not my_place:
                pltpu.make_async_remote_copy(
                    src_ref=gain_in.at[0, :, my_place],
                    dst_ref=gain_in.at[0, :, my_place],
                    send_sem=gain_send.at[0],
                    recv_sem=gain_recv.at[0, 0],
                    device_id=(band, my_slab * per_slab + place),
                    device_id_type=MESH,
                ).start()

    def receive_start():
        whole = gain_in.at[0, :, pl.ds(0, per_slab - 1)]
        pltpu.make_async_copy(whole, whole, gain_recv.at[0, 0]).wait()
        for order in range(tiles):
            unpack_tile(0, order)

    def receive_tile(slot, order):
        slab = near[order]
        whole = gain_in.at[slot, slab, pl.ds(0, per_slab - 1 if order == 0 else per_slab)]
        pltpu.make_async_copy(whole, whole, gain_recv.at[slot, slab]).wait()
        unpack_tile(slot, order)

    def unpack_tile(slot, order):
        slab = near[order]
        packed = gain_in[slot, slab].reshape(width, 128)
        value = lax.dot_general(fold, packed, NT, preferred_element_type=jnp.float32)
        columns[order] = value.reshape(columns.shape[1:])

    def send_mixed(slot, value):
        mixed_out[slot] = split(value)
        mixed_in[slot, band] = mixed_out[slot]

        for peer in bands:
            pltpu.make_async_remote_copy(
                src_ref=mixed_out.at[slot],
                dst_ref=mixed_in.at[slot, band],
                send_sem=mixed_send.at[slot],
                recv_sem=mixed_recv.at[slot],
                device_id=(peer, me),
                device_id_type=MESH,
            ).start()

    inverse = gram_inverse(n_band)
    own_place = (2.0 * band.astype(jnp.float32) + 1.0 - n_band) / n_band

    def receive_mixed(slot):
        whole = mixed_in.at[slot, pl.ds(0, n_band - 1)]
        pltpu.make_async_copy(whole, whole, mixed_recv.at[slot]).wait()
        totals = [None, None, None]
        for index in range(n_band):
            place = (2.0 * index + 1.0 - n_band) / n_band
            value = mixed_in[slot, index].astype(jnp.float32)
            for order in range(3):
                term = value * (place**order)
                totals[order] = term if totals[order] is None else totals[order] + term
        moments = [value + pltpu.roll(value, 2 * PART, 1) for value in totals]
        return [
            moments[0] * inverse[row][0] + moments[1] * inverse[row][1] + moments[2] * inverse[row][2]
            for row in range(3)
        ]

    small[0].wait()
    small[1].wait()
    live = lax.broadcasted_iota(jnp.int32, (1, sources), 1) < count[0]
    weight = jnp.where(live, flux[...], 0.0)

    def combine(by_re, by_im, begin_row, begin_col):
        count = by_re.shape[1]
        real = by_re[:width] + by_im[width:]
        imag = by_re[width:] - by_im[:width]
        off = (lax.broadcasted_iota(jnp.int32, (width, count), 0) + begin_row) != (
            lax.broadcasted_iota(jnp.int32, (width, count), 1) + begin_col
        )
        shape = (per_slab, own, count)
        return [jnp.where(off, value, 0.0).astype(jnp.bfloat16).reshape(shape) for value in (real, imag)]

    def left_rows(begin):
        return jnp.concatenate([resp[0, pl.ds(begin, width), :], resp[1, pl.ds(begin, width), :]], axis=0)

    def send_rows(first_dir):
        def send(place, inner):
            peer = first_dir + lax.rem(my_place + per_slab // 2 + place, per_slab)

            @pl.when(peer != me)
            def _():
                pltpu.make_async_remote_copy(
                    src_ref=coh_out.at[peer],
                    dst_ref=coh_in.at[me],
                    send_sem=coh_send,
                    recv_sem=coh_recv.at[me],
                    device_id=(band, peer),
                    device_id_type=MESH,
                ).start()

            return inner

        lax.fori_loop(0, per_slab, send, 0)

    far_begin = pl.multiple_of(slabs[0] * width, width)
    far_dirs = pl.ds(slabs[0] * per_slab, per_slab)
    for index, slab in enumerate(slabs):
        large[index].wait()
        begin = pl.multiple_of(slab * width, width)
        here = pl.ds(begin, width)
        pieces = []
        for part in range(2):
            piece = (resp[part, here, :].astype(jnp.float32) * weight).astype(jnp.bfloat16)
            scaled[pl.ds(pl.multiple_of(part * stations + begin, width), width), :] = piece
            pieces.append(piece)
        right = jnp.concatenate(pieces, axis=0)
        product = lax.dot_general(left_rows(far_begin), right, NT, preferred_element_type=jnp.float32)
        real, imag = combine(product[:, :width], product[:, width:], far_begin, begin)
        coh_out[far_dirs, 0, :, here] = real
        coh_out[far_dirs, 1, :, here] = imag
    pl.semaphore_wait(barrier, n_dir + n_band - 2)
    small[3].wait()
    strength = jnp.ones((own, 128), jnp.float32)
    for index in range(n_dir):
        strength = jnp.where(dir_lane == index, penalty[index], strength)

    small[2].wait()
    pieces = []
    for part in range(2):
        pieces.append(start[part])
        if n_dir < PART:
            pieces.append(jnp.zeros((own, PART - n_dir), jnp.float32))
    gains = jnp.concatenate(pieces + pieces, axis=1)

    send_start(gains)
    send_rows(slabs[0] * per_slab)

    def slab_step(step, carry):
        slab = lax.rem(my_slab + 2 + 3 * step + 3 * (step // 2) + 2 * (step // 3), SLABS)
        begin = pl.multiple_of(slab * width, width)
        left = left_rows(begin)
        by_re = lax.dot_general(left, scaled[:stations], NT, preferred_element_type=jnp.float32)
        by_im = lax.dot_general(left, scaled[stations:], NT, preferred_element_type=jnp.float32)
        first_dir = slab * per_slab
        real, imag = combine(by_re, by_im, begin, 0)
        coh_out[pl.ds(first_dir, per_slab), 0] = real
        coh_out[pl.ds(first_dir, per_slab), 1] = imag
        send_rows(first_dir)
        return carry

    lax.fori_loop(1, SLABS, slab_step, 0)
    coh_in[me] = coh_out[me]
    widen(gains)
    small[4].wait()
    row_id = lax.broadcasted_iota(jnp.int32, (own, stations), 0) + me * own
    col_id = lax.broadcasted_iota(jnp.int32, (own, stations), 1)
    for part in range(2):
        vis[part] = jnp.where(row_id == col_id, 0.0, vis[part])
    forward_start()

    def advance(index, group, member, order, totals):
        here = pl.ds(order * width, width)
        coh_re = coh[index, 0, :, here]
        coh_im = coh[index, 1, :, here]
        col_re = columns[order, group, member : member + 1]
        col_im = columns[order, PART // GROUP + group, member : member + 1]
        row_re = rows_wide[index]
        row_im = rows_wide[PART + index]
        along_re = coh_re * col_re + coh_im * col_im
        along_im = coh_im * col_re - coh_re * col_im
        along[index, 0, :, here] = along_re
        along[index, 1, :, here] = along_im
        return (
            totals[0] + (row_re * along_re - row_im * along_im),
            totals[1] + (row_re * along_im + row_im * along_re),
        )

    def left_over(order, totals):
        return vis[0, :, spans[order]] - totals[0], vis[1, :, spans[order]] - totals[1]

    def project_first():
        groups = n_dir // GROUP

        def step(turn, totals):
            group = lax.rem(me // GROUP + turn + turn // 2 - 2 * (turn // 3), groups)
            for member in range(GROUP):
                index = group * GROUP + member

                @pl.when(index != me)
                def _(index=index):
                    block = coh_in.at[index]
                    pltpu.make_async_copy(block, block, coh_recv.at[index]).wait()

                for order in range(tiles):
                    here = pl.ds(order * width, width)
                    for part in range(2):
                        coh[index, part, :, here] = coh_in[index, part, :, spans[order]].astype(jnp.float32)
                totals = tuple(
                    advance(index, group, member, order, totals[order]) for order in range(tiles)
                )
            return totals

        totals = lax.fori_loop(0, n_dir // GROUP, step, ((zero, zero),) * tiles)
        return [left_over(order, totals[order]) for order in range(tiles)]

    def project_tile(order):
        def step(group, totals):
            for member in range(GROUP):
                totals = advance(group * GROUP + member, group, member, order, totals)
            return totals

        return left_over(order, lax.fori_loop(0, n_dir // GROUP, step, (zero, zero)))

    def reduce(orders, residuals, opening, closing):
        def step(index, carry):
            if opening:
                total_re, total_im, total_weight = zero, zero, zero
            else:
                total_re, total_im, total_weight = sums[index, 0], sums[index, 1], sums[index, 2]
            for order, (residual_re, residual_im) in zip(orders, residuals):
                here = pl.ds(order * width, width)
                along_re = along[index, 0, :, here]
                along_im = along[index, 1, :, here]
                total_weight += along_re * along_re + along_im * along_im
                total_re += residual_re * along_re + residual_im * along_im
                total_im += residual_im * along_re - residual_re * along_im
            if not closing:
                sums[index, 0] = total_re
                sums[index, 1] = total_im
                sums[index, 2] = total_weight
                return carry
            numer, weights = carry
            sum_re = jnp.sum(total_re, axis=1, keepdims=True)
            sum_im = jnp.sum(total_im, axis=1, keepdims=True)
            sum_weight = jnp.sum(total_weight, axis=1, keepdims=True)
            numer = jnp.where(part_lane == index, sum_re, jnp.where(part_lane == PART + index, sum_im, numer))
            weights = jnp.where(dir_lane == index, sum_weight, weights)
            return numer, weights

        return lax.fori_loop(0, n_dir, step, (zero, zero), unroll=n_dir if closing else GROUP)

    def agree(slot, value, duals):
        coefficients = receive_mixed(slot)
        target = coefficients[0] + own_place * coefficients[1] + own_place * own_place * coefficients[2]
        return target, duals + value - target

    target = gains
    duals = zero
    for sweep in range(SWEEPS):
        if sweep == 0:
            receive_start()
            numer, weights = reduce(range(tiles), project_first(), True, True)
        else:
            for order in range(tiles):
                if order == tiles - 1:
                    target, duals = agree(sweep - 1, gains, duals)
                receive_tile(sweep, order)
                residual = project_tile(order)
                numer, weights = reduce([order], [residual], order == 0, order == tiles - 1)
        solved = (numer + gains * weights + strength * (target - duals)) / (weights + strength)
        gains = gains + DAMPING * (solved - gains)
        send_gains(sweep + 1, gains)
        send_mixed(sweep, gains + duals)
        widen(gains)
        if sweep == SWEEPS - 1:
            for part in range(2):
                gains_ref[0, part] = gains[:, part * PART : part * PART + n_dir]
    for order in range(tiles):
        if order == tiles - 1:
            coefficients = receive_mixed(SWEEPS - 1)
            for index in range(3):
                for part in range(2):
                    coeff_ref[index, part] = coefficients[index][:, part * PART : part * PART + n_dir]
        receive_tile(SWEEPS, order)
        residual = project_tile(order)
        for part in range(2):
            resid_ref[0, part, :, spans[order]] = residual[part]

    whole = coh_out.at[pl.ds(0, n_dir - 1)]
    pltpu.make_async_copy(whole, whole, coh_send).wait()
    for slot in range(SWEEPS + 1):
        for slab in range(SLABS):
            whole = gain_in.at[slot, slab, pl.ds(0, per_slab - 1 if slab == 0 else per_slab)]
            pltpu.make_async_copy(whole, whole, gain_send.at[slot]).wait()
    for slot in range(SWEEPS):
        whole = mixed_in.at[slot, pl.ds(0, n_band - 1)]
        pltpu.make_async_copy(whole, whole, mixed_send.at[slot]).wait()


def hand_over(*refs):
    for source, goal in zip(refs[:3], refs[3:]):
        goal[...] = source[...]


def on_device(n_band, n_dir, responses, fluxes, counts, penalty, visibilities, start_gains):
    stations, sources = responses.shape[3], responses.shape[4]
    own = stations // n_dir
    width = stations // SLABS
    per_slab = n_dir // SLABS
    hbm = pl.BlockSpec(memory_space=pltpu.HBM)
    vmem = pl.BlockSpec(memory_space=pltpu.VMEM)
    bf16, f32 = jnp.bfloat16, jnp.float32
    gains, coefficients, residual = pl.pallas_call(
        functools.partial(calibrate, n_band, n_dir),
        out_shape=(
            jax.ShapeDtypeStruct((1, 2, own, n_dir), f32),
            jax.ShapeDtypeStruct((3, 2, own, n_dir), f32),
            jax.ShapeDtypeStruct((1, 2, own, stations), f32),
        ),
        in_specs=[hbm] * 6,
        out_specs=(vmem, vmem, vmem),
        scratch_shapes=[
            pltpu.VMEM((2, stations, sources), bf16),
            pltpu.VMEM((1, sources), f32),
            pltpu.VMEM((2, own, stations), f32),
            pltpu.VMEM((2, own, n_dir), f32),
            pltpu.SMEM((1,), jnp.int32),
            pltpu.SMEM((n_dir,), f32),
            pltpu.VMEM((2 * stations, sources), bf16),
            pltpu.VMEM((n_dir, 2, own, stations), bf16),
            pltpu.VMEM((n_dir, 2, own, stations), bf16),
            pltpu.VMEM((n_dir, 2, own, stations), f32),
            pltpu.VMEM((n_dir, 2, own, stations), f32),
            pltpu.VMEM((SLABS, 2 * PART // GROUP, GROUP, width), f32),
            pltpu.VMEM((2 * PART, own, 128), f32),
            pltpu.VMEM((n_dir, 3, own, 128), f32),
            pltpu.VMEM((SWEEPS + 1, own, 128), bf16),
            pltpu.VMEM((SWEEPS + 1, SLABS, per_slab, own, 128), bf16),
            pltpu.VMEM((SWEEPS, own, 128), bf16),
            pltpu.VMEM((SWEEPS, n_band, own, 128), bf16),
            pltpu.SemaphoreType.DMA((SLABS + 5,)),
            pltpu.SemaphoreType.DMA,
            pltpu.SemaphoreType.DMA((n_dir,)),
            pltpu.SemaphoreType.DMA((SWEEPS + 1,)),
            pltpu.SemaphoreType.DMA((SWEEPS + 1, SLABS)),
            pltpu.SemaphoreType.DMA,
            pltpu.SemaphoreType.DMA((SWEEPS,)),
            pltpu.SemaphoreType.DMA((SWEEPS,)),
        ],
        compiler_params=pltpu.CompilerParams(
            collective_id=0, has_side_effects=True, vmem_limit_bytes=40 * 1024 * 1024
        ),
    )(
        *[pltpu.with_memory_space_constraint(value, pltpu.HBM) for value in (responses, fluxes)],
        counts,
        pltpu.with_memory_space_constraint(penalty, pltpu.HBM),
        pltpu.with_memory_space_constraint(visibilities, pltpu.HBM),
        pltpu.with_memory_space_constraint(jnp.transpose(start_gains, (0, 1, 3, 2)), pltpu.HBM),
    )
    results = (gains, coefficients, residual)
    gains, coefficients, residual = pl.pallas_call(
        hand_over,
        out_shape=tuple(jax.ShapeDtypeStruct(value.shape, value.dtype) for value in results),
        in_specs=[vmem] * 3,
        out_specs=(vmem,) * 3,
        compiler_params=pltpu.CompilerParams(vmem_limit_bytes=4 * 1024 * 1024),
    )(*results)
    return jnp.transpose(gains, (0, 1, 3, 2)), jnp.transpose(coefficients, (0, 1, 3, 2)), residual


def solution(mesh):
    in_specs = (
        P("band", "dir", None, None, None),
        P("band", "dir", None),
        P("dir"),
        P(),
        P("band", None, "dir", None),
        P("band", None, None, "dir"),
    )
    out_specs = (
        P("band", None, None, "dir"),
        P(None, None, None, "dir"),
        P("band", None, "dir", None),
    )
    return jax.shard_map(
        functools.partial(on_device, mesh.shape["band"], mesh.shape["dir"]),
        mesh=mesh,
        in_specs=in_specs,
        out_specs=out_specs,
        check_vma=False,
    )
```

```python
import functools

import jax
import jax.numpy as jnp
from jax import lax
from jax.experimental import pallas as pl
from jax.experimental.pallas import tpu as pltpu
from jax.sharding import PartitionSpec as P

MESH = pl.DeviceIdType.MESH
SWEEPS = 3
RIDGE_WEIGHT = 0.25
DAMPING = 0.5
SLABS = 4
PART = 32
GROUP = 8
NT = (((1,), (1,)), ((), ()))


def gram_inverse(band_total):
    locations = [(2.0 * position + 1.0 - band_total) / band_total for position in range(band_total)]
    gram = [
        [
            sum((location ** (first + second) for location in locations))
            + (RIDGE_WEIGHT if first == second else 0.0)
            for second in range(3)
        ]
        for first in range(3)
    ]

    def cofactor(first, second):
        rows = [index for index in range(3) if index != first]
        cols = [index for index in range(3) if index != second]
        minor = gram[rows[0]][cols[0]] * gram[rows[1]][cols[1]] - gram[rows[0]][cols[1]] * gram[rows[1]][cols[0]]
        return minor if (first + second) % 2 == 0 else -minor

    determinant = sum((gram[0][column] * cofactor(0, column) for column in range(3)))
    return [[cofactor(column, row) / determinant for column in range(3)] for row in range(3)]


def calibrate(
    n_band,
    n_dir,
    resp_hbm,
    flux_hbm,
    count_hbm,
    penalty_hbm,
    vis_hbm,
    start_hbm,
    gains_ref,
    coeff_ref,
    resid_ref,
    resp,
    flux,
    vis,
    start,
    count,
    penalty,
    scaled,
    coh_out,
    coh_in,
    coh,
    along,
    columns,
    rows_wide,
    sums,
    gain_out,
    gain_in,
    mixed_out,
    mixed_in,
    load_sem,
    coh_send,
    coh_recv,
    gain_send,
    gain_recv,
    start_recv,
    mixed_send,
    mixed_recv,
):
    me = lax.axis_index("dir")
    band = lax.axis_index("band")
    stations, sources = resp.shape[1], resp.shape[2]
    per_slab = n_dir // SLABS
    own = stations // n_dir
    tiles = SLABS
    width = stations // SLABS
    my_slab = me // per_slab
    my_place = lax.rem(me, per_slab)

    slabs = [lax.rem(my_slab + offset, SLABS) for offset in (2, 1, 3, 0)]
    chunks = [pl.ds(pl.multiple_of(slab * width, width), width) for slab in slabs]
    small = [
        pltpu.make_async_copy(source, goal, load_sem.at[SLABS + index])
        for index, (source, goal) in enumerate(
            (
                (flux_hbm.at[0], flux),
                (count_hbm, count),
                (start_hbm.at[0], start),
                (penalty_hbm, penalty),
                (vis_hbm.at[0], vis),
            )
        )
    ]
    large = [
        pltpu.make_async_copy(resp_hbm.at[0, 0, :, rows], resp.at[:, rows], load_sem.at[index])
        for index, rows in enumerate(chunks)
    ]
    for load in small[:1] + large:
        load.start()

    barrier = pltpu.get_barrier_semaphore()

    rotations = [step for step in (4, 5, 2, 3, 6, 7, 1, 0) if step < per_slab]
    places = [my_place if step == 0 else lax.rem(my_place + step, per_slab) for step in rotations]
    peers = []
    for offset in (2, 1, 3, 0):
        slab = lax.rem(my_slab + offset, SLABS)
        for step, place in zip(rotations, places):
            if offset or step:
                peers.append(slab * per_slab + place)
    bands = [lax.rem(band + step, n_band) for step in range(1, n_band)]
    for peer in peers:
        pl.semaphore_signal(barrier, inc=1, device_id=(band, peer), device_id_type=MESH)
    for peer in bands:
        pl.semaphore_signal(barrier, inc=1, device_id=(peer, me), device_id_type=MESH)
    for load in small[1:]:
        load.start()

    lane = lax.broadcasted_iota(jnp.int32, (own, 128), 1)
    dir_lane = lane % PART
    part_lane = lane % (2 * PART)
    low_half = lane < 2 * PART
    fold = (
        lax.broadcasted_iota(jnp.int32, (2 * PART, 128), 0)
        == lax.broadcasted_iota(jnp.int32, (2 * PART, 128), 1) % (2 * PART)
    ).astype(jnp.bfloat16)
    zero = jnp.zeros((own, 128), jnp.float32)

    def split(value):
        high = value.astype(jnp.bfloat16).astype(jnp.float32)
        return jnp.where(low_half, high, value - high).astype(jnp.bfloat16)

    near = [lax.rem(my_slab + offset, SLABS) for offset in (0, 1, 3, 2)]
    spans = [pl.ds(pl.multiple_of(slab * width, width), width) for slab in near]

    def widen(value):
        for part in range(2):
            for index in range(n_dir):
                place = part * PART + index
                rows_wide[place] = jnp.broadcast_to(value[:, place : place + 1], (own, 128))

    def send_gains(slot, value):
        gain_out[slot] = split(value)
        gain_in[slot, my_slab, my_place] = gain_out[slot]

        for peer in peers:
            pltpu.make_async_remote_copy(
                src_ref=gain_out.at[slot],
                dst_ref=gain_in.at[slot, my_slab, my_place],
                send_sem=gain_send.at[slot],
                recv_sem=gain_recv.at[slot, my_slab],
                device_id=(band, peer),
                device_id_type=MESH,
            ).start()

    def send_start(gains):
        gain_out[0] = split(gains)
        gain_in[0, my_slab, my_place] = gain_out[0]
        for offset in (2, 1, 3):
            pltpu.make_async_remote_copy(
                src_ref=gain_out.at[0],
                dst_ref=gain_in.at[0, my_slab, my_place],
                send_sem=gain_send.at[0],
                recv_sem=start_recv,
                device_id=(band, lax.rem(my_slab + offset, SLABS) * per_slab + my_place),
                device_id_type=MESH,
            ).start()

    def forward_start():
        whole = gain_in.at[0, pl.ds(0, SLABS - 1), 0]
        pltpu.make_async_copy(whole, whole, start_recv).wait()
        for place in places:
            if place is not my_place:
                pltpu.make_async_remote_copy(
                    src_ref=gain_in.at[0, :, my_place],
                    dst_ref=gain_in.at[0, :, my_place],
                    send_sem=gain_send.at[0],
                    recv_sem=gain_recv.at[0, 0],
                    device_id=(band, my_slab * per_slab + place),
                    device_id_type=MESH,
                ).start()

    def receive_start():
        whole = gain_in.at[0, :, pl.ds(0, per_slab - 1)]
        pltpu.make_async_copy(whole, whole, gain_recv.at[0, 0]).wait()
        for order in range(tiles):
            unpack_tile(0, order)

    def receive_tile(slot, order):
        slab = near[order]
        whole = gain_in.at[slot, slab, pl.ds(0, per_slab - 1 if order == 0 else per_slab)]
        pltpu.make_async_copy(whole, whole, gain_recv.at[slot, slab]).wait()
        unpack_tile(slot, order)

    def unpack_tile(slot, order):
        slab = near[order]
        packed = gain_in[slot, slab].reshape(width, 128)
        value = lax.dot_general(fold, packed, NT, preferred_element_type=jnp.float32)
        columns[order] = value.reshape(columns.shape[1:])

    def send_mixed(slot, value):
        mixed_out[slot] = split(value)
        mixed_in[slot, band] = mixed_out[slot]

        for peer in bands:
            pltpu.make_async_remote_copy(
                src_ref=mixed_out.at[slot],
                dst_ref=mixed_in.at[slot, band],
                send_sem=mixed_send.at[slot],
                recv_sem=mixed_recv.at[slot],
                device_id=(peer, me),
                device_id_type=MESH,
            ).start()

    inverse = gram_inverse(n_band)
    own_place = (2.0 * band.astype(jnp.float32) + 1.0 - n_band) / n_band

    def receive_mixed(slot):
        whole = mixed_in.at[slot, pl.ds(0, n_band - 1)]
        pltpu.make_async_copy(whole, whole, mixed_recv.at[slot]).wait()
        totals = [None, None, None]
        for index in range(n_band):
            place = (2.0 * index + 1.0 - n_band) / n_band
            value = mixed_in[slot, index].astype(jnp.float32)
            for order in range(3):
                term = value * (place**order)
                totals[order] = term if totals[order] is None else totals[order] + term
        moments = [value + pltpu.roll(value, 2 * PART, 1) for value in totals]
        return [
            moments[0] * inverse[row][0] + moments[1] * inverse[row][1] + moments[2] * inverse[row][2]
            for row in range(3)
        ]

    small[0].wait()
    small[1].wait()
    live = lax.broadcasted_iota(jnp.int32, (1, sources), 1) < count[0]
    weight = jnp.where(live, flux[...], 0.0)

    def combine(by_re, by_im, begin_row, begin_col):
        count = by_re.shape[1]
        real = by_re[:width] + by_im[width:]
        imag = by_re[width:] - by_im[:width]
        off = (lax.broadcasted_iota(jnp.int32, (width, count), 0) + begin_row) != (
            lax.broadcasted_iota(jnp.int32, (width, count), 1) + begin_col
        )
        shape = (per_slab, own, count)
        return [jnp.where(off, value, 0.0).astype(jnp.bfloat16).reshape(shape) for value in (real, imag)]

    def left_rows(begin):
        return jnp.concatenate([resp[0, pl.ds(begin, width), :], resp[1, pl.ds(begin, width), :]], axis=0)

    def send_rows(first_dir):
        def send(place, inner):
            peer = first_dir + lax.rem(my_place + per_slab // 2 + place, per_slab)

            @pl.when(peer != me)
            def _():
                pltpu.make_async_remote_copy(
                    src_ref=coh_out.at[peer],
                    dst_ref=coh_in.at[me],
                    send_sem=coh_send,
                    recv_sem=coh_recv.at[me],
                    device_id=(band, peer),
                    device_id_type=MESH,
                ).start()

            return inner

        lax.fori_loop(0, per_slab, send, 0)

    far_begin = pl.multiple_of(slabs[0] * width, width)
    far_dirs = pl.ds(slabs[0] * per_slab, per_slab)
    for index, slab in enumerate(slabs):
        large[index].wait()
        begin = pl.multiple_of(slab * width, width)
        here = pl.ds(begin, width)
        pieces = []
        for part in range(2):
            piece = (resp[part, here, :].astype(jnp.float32) * weight).astype(jnp.bfloat16)
            scaled[pl.ds(pl.multiple_of(part * stations + begin, width), width), :] = piece
            pieces.append(piece)
        right = jnp.concatenate(pieces, axis=0)
        product = lax.dot_general(left_rows(far_begin), right, NT, preferred_element_type=jnp.float32)
        real, imag = combine(product[:, :width], product[:, width:], far_begin, begin)
        coh_out[far_dirs, 0, :, here] = real
        coh_out[far_dirs, 1, :, here] = imag
    pl.semaphore_wait(barrier, n_dir + n_band - 2)
    small[3].wait()
    strength = jnp.ones((own, 128), jnp.float32)
    for index in range(n_dir):
        strength = jnp.where(dir_lane == index, penalty[index], strength)

    small[2].wait()
    pieces = []
    for part in range(2):
        pieces.append(start[part])
        if n_dir < PART:
            pieces.append(jnp.zeros((own, PART - n_dir), jnp.float32))
    gains = jnp.concatenate(pieces + pieces, axis=1)

    send_start(gains)
    send_rows(slabs[0] * per_slab)

    def slab_step(step, carry):
        slab = lax.rem(my_slab + 2 + 3 * step + 3 * (step // 2) + 2 * (step // 3), SLABS)
        begin = pl.multiple_of(slab * width, width)
        left = left_rows(begin)
        by_re = lax.dot_general(left, scaled[:stations], NT, preferred_element_type=jnp.float32)
        by_im = lax.dot_general(left, scaled[stations:], NT, preferred_element_type=jnp.float32)
        first_dir = slab * per_slab
        real, imag = combine(by_re, by_im, begin, 0)
        coh_out[pl.ds(first_dir, per_slab), 0] = real
        coh_out[pl.ds(first_dir, per_slab), 1] = imag
        send_rows(first_dir)
        return carry

    lax.fori_loop(1, SLABS, slab_step, 0)
    coh_in[me] = coh_out[me]
    widen(gains)
    small[4].wait()
    row_id = lax.broadcasted_iota(jnp.int32, (own, stations), 0) + me * own
    col_id = lax.broadcasted_iota(jnp.int32, (own, stations), 1)
    for part in range(2):
        vis[part] = jnp.where(row_id == col_id, 0.0, vis[part])
    forward_start()

    def advance(index, group, member, order, totals, keep=True):
        here = pl.ds(order * width, width)
        coh_re = coh[index, 0, :, here]
        coh_im = coh[index, 1, :, here]
        col_re = columns[order, group, member : member + 1]
        col_im = columns[order, PART // GROUP + group, member : member + 1]
        row_re = rows_wide[index]
        row_im = rows_wide[PART + index]
        along_re = coh_re * col_re + coh_im * col_im
        along_im = coh_im * col_re - coh_re * col_im
        if keep:
            along[index, 0, :, here] = along_re
            along[index, 1, :, here] = along_im
        return (
            totals[0] + (row_re * along_re - row_im * along_im),
            totals[1] + (row_re * along_im + row_im * along_re),
        )

    def left_over(order, totals):
        return vis[0, :, spans[order]] - totals[0], vis[1, :, spans[order]] - totals[1]

    def project_first():
        groups = n_dir // GROUP

        def step(turn, totals):
            group = lax.rem(me // GROUP + turn + turn // 2 - 2 * (turn // 3), groups)
            for member in range(GROUP):
                index = group * GROUP + member

                @pl.when(index != me)
                def _(index=index):
                    block = coh_in.at[index]
                    pltpu.make_async_copy(block, block, coh_recv.at[index]).wait()

                for order in range(tiles):
                    here = pl.ds(order * width, width)
                    for part in range(2):
                        coh[index, part, :, here] = coh_in[index, part, :, spans[order]].astype(jnp.float32)
                totals = tuple(
                    advance(index, group, member, order, totals[order]) for order in range(tiles)
                )
            return totals

        totals = lax.fori_loop(0, n_dir // GROUP, step, ((zero, zero),) * tiles)
        return [left_over(order, totals[order]) for order in range(tiles)]

    def project_tile(order, keep=True):
        def step(group, totals):
            for member in range(GROUP):
                totals = advance(group * GROUP + member, group, member, order, totals, keep)
            return totals

        return left_over(order, lax.fori_loop(0, n_dir // GROUP, step, (zero, zero)))

    def reduce(orders, residuals, opening, closing):
        def step(index, carry):
            if opening:
                total_re, total_im, total_weight = zero, zero, zero
            else:
                total_re, total_im, total_weight = sums[index, 0], sums[index, 1], sums[index, 2]
            for order, (residual_re, residual_im) in zip(orders, residuals):
                here = pl.ds(order * width, width)
                along_re = along[index, 0, :, here]
                along_im = along[index, 1, :, here]
                total_weight += along_re * along_re + along_im * along_im
                total_re += residual_re * along_re + residual_im * along_im
                total_im += residual_im * along_re - residual_re * along_im
            if not closing:
                sums[index, 0] = total_re
                sums[index, 1] = total_im
                sums[index, 2] = total_weight
                return carry
            numer, weights = carry
            sum_re = jnp.sum(total_re, axis=1, keepdims=True)
            sum_im = jnp.sum(total_im, axis=1, keepdims=True)
            sum_weight = jnp.sum(total_weight, axis=1, keepdims=True)
            numer = jnp.where(part_lane == index, sum_re, jnp.where(part_lane == PART + index, sum_im, numer))
            weights = jnp.where(dir_lane == index, sum_weight, weights)
            return numer, weights

        return lax.fori_loop(0, n_dir, step, (zero, zero), unroll=n_dir if closing else GROUP)

    def agree(slot, value, duals):
        coefficients = receive_mixed(slot)
        target = coefficients[0] + own_place * coefficients[1] + own_place * own_place * coefficients[2]
        return target, duals + value - target

    target = gains
    duals = zero
    for sweep in range(SWEEPS):
        if sweep == 0:
            receive_start()
            numer, weights = reduce(range(tiles), project_first(), True, True)
        else:
            for order in range(tiles):
                if order == tiles - 1:
                    target, duals = agree(sweep - 1, gains, duals)
                receive_tile(sweep, order)
                residual = project_tile(order)
                numer, weights = reduce([order], [residual], order == 0, order == tiles - 1)
        solved = (numer + gains * weights + strength * (target - duals)) / (weights + strength)
        gains = gains + DAMPING * (solved - gains)
        send_gains(sweep + 1, gains)
        send_mixed(sweep, gains + duals)
        widen(gains)
        if sweep == SWEEPS - 1:
            for part in range(2):
                gains_ref[0, part] = gains[:, part * PART : part * PART + n_dir]
    for order in range(tiles):
        if order == tiles - 1:
            coefficients = receive_mixed(SWEEPS - 1)
            for index in range(3):
                for part in range(2):
                    coeff_ref[index, part] = coefficients[index][:, part * PART : part * PART + n_dir]
        receive_tile(SWEEPS, order)
        residual = project_tile(order, keep=False)
        for part in range(2):
            resid_ref[0, part, :, spans[order]] = residual[part]

    whole = coh_out.at[pl.ds(0, n_dir - 1)]
    pltpu.make_async_copy(whole, whole, coh_send).wait()
    for slot in range(SWEEPS + 1):
        for slab in range(SLABS):
            whole = gain_in.at[slot, slab, pl.ds(0, per_slab - 1 if slab == 0 else per_slab)]
            pltpu.make_async_copy(whole, whole, gain_send.at[slot]).wait()
    for slot in range(SWEEPS):
        whole = mixed_in.at[slot, pl.ds(0, n_band - 1)]
        pltpu.make_async_copy(whole, whole, mixed_send.at[slot]).wait()


def hand_over(*refs):
    for source, goal in zip(refs[:3], refs[3:]):
        goal[...] = source[...]


def on_device(n_band, n_dir, responses, fluxes, counts, penalty, visibilities, start_gains):
    stations, sources = responses.shape[3], responses.shape[4]
    own = stations // n_dir
    width = stations // SLABS
    per_slab = n_dir // SLABS
    hbm = pl.BlockSpec(memory_space=pltpu.HBM)
    vmem = pl.BlockSpec(memory_space=pltpu.VMEM)
    bf16, f32 = jnp.bfloat16, jnp.float32
    gains, coefficients, residual = pl.pallas_call(
        functools.partial(calibrate, n_band, n_dir),
        out_shape=(
            jax.ShapeDtypeStruct((1, 2, own, n_dir), f32),
            jax.ShapeDtypeStruct((3, 2, own, n_dir), f32),
            jax.ShapeDtypeStruct((1, 2, own, stations), f32),
        ),
        in_specs=[hbm] * 6,
        out_specs=(vmem, vmem, vmem),
        scratch_shapes=[
            pltpu.VMEM((2, stations, sources), bf16),
            pltpu.VMEM((1, sources), f32),
            pltpu.VMEM((2, own, stations), f32),
            pltpu.VMEM((2, own, n_dir), f32),
            pltpu.SMEM((1,), jnp.int32),
            pltpu.SMEM((n_dir,), f32),
            pltpu.VMEM((2 * stations, sources), bf16),
            pltpu.VMEM((n_dir, 2, own, stations), bf16),
            pltpu.VMEM((n_dir, 2, own, stations), bf16),
            pltpu.VMEM((n_dir, 2, own, stations), f32),
            pltpu.VMEM((n_dir, 2, own, stations), f32),
            pltpu.VMEM((SLABS, 2 * PART // GROUP, GROUP, width), f32),
            pltpu.VMEM((2 * PART, own, 128), f32),
            pltpu.VMEM((n_dir, 3, own, 128), f32),
            pltpu.VMEM((SWEEPS + 1, own, 128), bf16),
            pltpu.VMEM((SWEEPS + 1, SLABS, per_slab, own, 128), bf16),
            pltpu.VMEM((SWEEPS, own, 128), bf16),
            pltpu.VMEM((SWEEPS, n_band, own, 128), bf16),
            pltpu.SemaphoreType.DMA((SLABS + 5,)),
            pltpu.SemaphoreType.DMA,
            pltpu.SemaphoreType.DMA((n_dir,)),
            pltpu.SemaphoreType.DMA((SWEEPS + 1,)),
            pltpu.SemaphoreType.DMA((SWEEPS + 1, SLABS)),
            pltpu.SemaphoreType.DMA,
            pltpu.SemaphoreType.DMA((SWEEPS,)),
            pltpu.SemaphoreType.DMA((SWEEPS,)),
        ],
        compiler_params=pltpu.CompilerParams(
            collective_id=0, has_side_effects=True, vmem_limit_bytes=40 * 1024 * 1024
        ),
    )(
        *[pltpu.with_memory_space_constraint(value, pltpu.HBM) for value in (responses, fluxes)],
        counts,
        pltpu.with_memory_space_constraint(penalty, pltpu.HBM),
        pltpu.with_memory_space_constraint(visibilities, pltpu.HBM),
        pltpu.with_memory_space_constraint(jnp.transpose(start_gains, (0, 1, 3, 2)), pltpu.HBM),
    )
    results = (gains, coefficients, residual)
    gains, coefficients, residual = pl.pallas_call(
        hand_over,
        out_shape=tuple(jax.ShapeDtypeStruct(value.shape, value.dtype) for value in results),
        in_specs=[vmem] * 3,
        out_specs=(vmem,) * 3,
        compiler_params=pltpu.CompilerParams(vmem_limit_bytes=4 * 1024 * 1024),
    )(*results)
    return jnp.transpose(gains, (0, 1, 3, 2)), jnp.transpose(coefficients, (0, 1, 3, 2)), residual


def solution(mesh):
    in_specs = (
        P("band", "dir", None, None, None),
        P("band", "dir", None),
        P("dir"),
        P(),
        P("band", None, "dir", None),
        P("band", None, None, "dir"),
    )
    out_specs = (
        P("band", None, None, "dir"),
        P(None, None, None, "dir"),
        P("band", None, "dir", None),
    )
    return jax.shard_map(
        functools.partial(on_device, mesh.shape["band"], mesh.shape["dir"]),
        mesh=mesh,
        in_specs=in_specs,
        out_specs=out_specs,
        check_vma=False,
    )
```
